256 devices in a mesh: grp: 4 (over y), sp: 64 (over z, x, core).
Axes of the slice: x: 4, y: 4, z: 8, core: 2. Of those that a mesh axis runs over, the one named last changes fastest.
Arguments:
- query: bfloat16 [32768, 768], P(('grp', 'sp')), may hold values from -32 to 32
- key_in: bfloat16 [32768, 768], P(('grp', 'sp')), may hold values from -8 to 8
- value: bfloat16 [32768, 768], P(('grp', 'sp')), may hold values from -6 to 6
- lengths: int32 [4, 8], P('grp'), may hold values from 0 to 8192, as said below
- kernel: bfloat16 [31, 768], replicated, may hold values from -2 to 2
- cotangent: bfloat16 [32768, 768], P(('grp', 'sp')), may hold values from -6 to 6
Outputs:
- output: bfloat16 [32768, 768], P(('grp', 'sp'))
- query_grad: bfloat16 [32768, 768], P(('grp', 'sp'))
- key_grad: bfloat16 [32768, 768], P(('grp', 'sp'))
- value_grad: bfloat16 [32768, 768], P(('grp', 'sp'))
- kernel_grad: float32 [31, 768], replicated
The draws below stay inside these ranges and needn't reach their ends.
Inputs may be any that keep to these rules, and one draw needn't show every extreme that they name: `lengths`: each row sums to 8192; entries are multiples of 1024, the nonzero ones first; row 0 is one recording of all 8192 frames.
All inputs are finite; a program needn't handle non-finite values.
Results may differ from the reference program's by a relative error of at most 0.015.
The reference program's roundings to bfloat16 on the way count: a program that leaves them out, or rounds other values in their place, can miss the bound.
Values may be sent and summed in bfloat16 or wider, within the bound.
No kernel may reach another device: no remote copies, remote signals or barrier semaphores. Data moves between devices by JAX's collectives and lax.ppermute only.
A program may use at most 128 MiB of HBM per device.

```python
import math
import jax
import jax.numpy as jnp
from jax import lax

FR_DEV = 128
HEADS = 8
HEAD_DIM = 96
KERNEL = 31
RECS = 8
CHANNELS = 768
FRAMES = 32768
N_GRP = 4
N_SP = 64


def draw_query(key, part):
    key = jax.random.fold_in(key, 1)
    result = jnp.clip(1.3 * jax.random.normal(key, (FRAMES, HEADS * HEAD_DIM), jnp.float32), -7.8, 7.8)
    return result.astype(jnp.bfloat16)


def draw_key_in(key, part):
    key = jax.random.fold_in(key, 2)
    result = jnp.clip(1.3 * jax.random.normal(key, (FRAMES, HEADS * HEAD_DIM), jnp.float32), -7.8, 7.8)
    return result.astype(jnp.bfloat16)


def draw_lengths(key, part):
    key = jax.random.fold_in(key, 3)
    cuts = jax.random.randint(key, (N_GRP, RECS - 1), 0, 2).astype(jnp.int32)
    cuts = cuts * (jnp.arange(N_GRP) > 0).astype(jnp.int32)[:, None]
    spots = jnp.arange(1, RECS, dtype=jnp.int32)[None, :]
    ends = jnp.sort(jnp.where(cuts > 0, spots, RECS), axis=1).astype(jnp.int32)
    ends = jnp.concatenate([ends, jnp.full((N_GRP, 1), RECS, jnp.int32)], axis=1)
    starts = jnp.concatenate([jnp.zeros((N_GRP, 1), jnp.int32), ends[:, :-1]], axis=1)
    return ((ends - starts) * (FR_DEV * N_SP // RECS)).astype(jnp.int32)


def block_scale(stream_key, shape, cuts, low, top_value):
    def one(axis_at, blocks):
        heights = jax.random.uniform(jax.random.fold_in(jax.random.fold_in(stream_key, 6), axis_at), (blocks,), jnp.float32, low / len(cuts), top_value / len(cuts))
        return jnp.repeat(jnp.exp(heights), shape[axis_at] // blocks).reshape((-1,) + (1,) * (len(shape) - axis_at - 1))

    level = one(*cuts[0])
    for cut in cuts[1:]:
        level = level * one(*cut)
    return level


def centred(rng, dims, deviation, most, shards=(), kind=jnp.bfloat16):
    values = deviation * jax.random.normal(rng, dims, jnp.float32)
    if shards:
        values = values * block_scale(rng, dims, shards, -0.22, 0.18)
    return jnp.clip(values, -most, most).astype(kind)


def setup_inputs(seed: int = 0) -> dict:
    arg_keys = jax.random.split(jax.random.key(seed), 7)
    query = draw_query(jax.random.fold_in(arg_keys[6], 71), 0)
    key_in = draw_key_in(jax.random.fold_in(arg_keys[6], 71), 0)
    value = centred(arg_keys[2], (FRAMES, CHANNELS), 1.0, 6.0, ((0, 256),))
    lengths = draw_lengths(jax.random.fold_in(arg_keys[6], 71), 0)
    kernel = centred(arg_keys[4], (KERNEL, CHANNELS), 0.35, 2.0)
    cotangent = centred(arg_keys[5], (FRAMES, CHANNELS), 1.0, 6.0, ((0, 256),))
    return {"query": query, "key_in": key_in, "value": value, "lengths": lengths, "kernel": kernel, "cotangent": cotangent}


masked_value = -1.0e30


def segment_of(positions, lengths_row):
    ends = jnp.cumsum(lengths_row).astype(jnp.int32)
    return jnp.sum((positions[:, None] >= ends[None, :]).astype(jnp.int32), axis=1).astype(jnp.int32)


def head_forward(query_head, key_head, value_head, query_seg, key_seg, scale):
    def block(inputs):
        rows_q, rows_seg = inputs
        scores = jnp.dot(rows_q, key_head.T, preferred_element_type=jnp.float32) * scale
        scores = jnp.where(rows_seg[:, None] == key_seg[None, :], scores, masked_value)
        peak = jnp.max(scores, axis=1, keepdims=True)
        weights = jnp.exp(scores - peak)
        total = jnp.sum(weights, axis=1)
        context = jnp.dot(weights.astype(jnp.bfloat16), value_head, preferred_element_type=jnp.float32)
        context = (context / total[:, None]).astype(jnp.bfloat16)
        return context, peak[:, 0] + jnp.log(total)
    return lax.map(block, (query_head, query_seg))


def head_backward(query_head, key_head, value_head, grad_head, lse_head, delta_head, query_seg, key_seg, scale):
    def block(carry, inputs):
        key_acc, value_acc = carry
        rows_q, rows_seg, rows_grad, rows_lse, rows_delta = inputs
        scores = jnp.dot(rows_q, key_head.T, preferred_element_type=jnp.float32) * scale
        scores = jnp.where(rows_seg[:, None] == key_seg[None, :], scores, masked_value)
        probs = jnp.exp(scores - rows_lse[:, None])
        probs_low = probs.astype(jnp.bfloat16)
        value_acc = value_acc + jnp.dot(probs_low.T, rows_grad, preferred_element_type=jnp.float32)
        prob_grad = jnp.dot(rows_grad, value_head.T, preferred_element_type=jnp.float32)
        score_grad = (probs * (prob_grad - rows_delta[:, None])).astype(jnp.bfloat16)
        query_part = jnp.dot(score_grad, key_head, preferred_element_type=jnp.float32) * scale
        key_acc = key_acc + jnp.dot(score_grad.T, rows_q, preferred_element_type=jnp.float32) * scale
        return (key_acc, value_acc), query_part
    empty = jnp.zeros(key_head.shape, jnp.float32)
    (key_acc, value_acc), query_part = lax.scan(block, (empty, empty), (query_head, query_seg, grad_head, lse_head, delta_head))
    return query_part, key_acc, value_acc


def reference(query, key_in, value, lengths, kernel, cotangent):
    line = FR_DEV * N_SP
    heads = HEADS
    channels = HEADS * HEAD_DIM
    scale = HEAD_DIM ** -0.5
    reach = KERNEL // 2
    block_rows = math.gcd(line, 1024)
    blocks = line // block_rows
    taps = kernel.astype(jnp.float32)
    outputs, query_grads, key_grads, value_grads = [], [], [], []
    kernel_total = jnp.zeros((KERNEL, channels), jnp.float32)
    for index in range(N_GRP):
        lengths_row = lengths[index]
        frame_ids = jnp.arange(line, dtype=jnp.int32)
        seg = segment_of(frame_ids, lengths_row)

        def split_heads(array):
            return array[index * line:(index + 1) * line].reshape(line, heads, HEAD_DIM).transpose(1, 0, 2)

        q_heads = split_heads(query)
        k_heads = split_heads(key_in)
        v_heads = split_heads(value)
        seg_blocks = seg.reshape(blocks, block_rows)

        def forward_one(inputs):
            q_one, k_one, v_one = inputs
            return head_forward(q_one.reshape(blocks, block_rows, HEAD_DIM), k_one, v_one, seg_blocks, seg, scale)

        ctx_heads, lse_heads = lax.map(forward_one, (q_heads, k_heads, v_heads))
        context = ctx_heads.reshape(heads, line, HEAD_DIM).transpose(1, 0, 2).reshape(line, channels)
        lse_heads = lse_heads.reshape(heads, line)

        padded = jnp.pad(context.astype(jnp.float32), ((reach, reach), (0, 0)))
        pad_pos = jnp.arange(line + 2 * reach, dtype=jnp.int32) - reach
        inside = (pad_pos >= 0) & (pad_pos < line)
        pad_seg = jnp.where(inside, segment_of(pad_pos, lengths_row), -1)
        conv = jnp.zeros((line, channels), jnp.float32)
        for offset in range(KERNEL):
            match = (pad_seg[offset:offset + line] == seg).astype(jnp.float32)[:, None]
            conv = conv + taps[offset] * padded[offset:offset + line] * match
        gate = jax.nn.sigmoid(conv)
        outputs.append((context.astype(jnp.float32) + conv * gate).astype(jnp.bfloat16))
        grad_out = cotangent[index * line:(index + 1) * line].astype(jnp.float32)
        conv_grad = grad_out * gate * (1.0 + conv * (1.0 - gate))
        rows_taps = []
        for offset in range(KERNEL):
            match = (pad_seg[offset:offset + line] == seg).astype(jnp.float32)[:, None]
            rows_taps.append(jnp.sum(conv_grad * padded[offset:offset + line] * match, axis=0))
        kernel_total = kernel_total + jnp.stack(rows_taps)
        grad_pad = jnp.pad(conv_grad, ((reach, reach), (0, 0)))
        context_grad = grad_out
        for offset in range(KERNEL):
            start = 2 * reach - offset
            match = (pad_seg[start:start + line] == seg).astype(jnp.float32)[:, None]
            context_grad = context_grad + taps[offset] * grad_pad[start:start + line] * match
        context_grad = context_grad.astype(jnp.bfloat16)
        delta = jnp.sum((context_grad.astype(jnp.float32) * context.astype(jnp.float32)).reshape(line, heads, HEAD_DIM), axis=2)
        g_heads = context_grad.reshape(line, heads, HEAD_DIM).transpose(1, 0, 2)

        def backward_one(inputs):
            q_one, k_one, v_one, g_one, lse_one, delta_one = inputs
            return head_backward(q_one.reshape(blocks, block_rows, HEAD_DIM), k_one, v_one,
                                 g_one.reshape(blocks, block_rows, HEAD_DIM), lse_one.reshape(blocks, block_rows),
                                 delta_one.reshape(blocks, block_rows), seg_blocks, seg, scale)

        dq_heads, dk_heads, dv_heads = lax.map(backward_one, (q_heads, k_heads, v_heads, g_heads, lse_heads, delta.T))

        def join(array):
            return array.reshape(heads, line, HEAD_DIM).transpose(1, 0, 2).reshape(line, channels).astype(jnp.bfloat16)

        query_grads.append(join(dq_heads))
        key_grads.append(join(dk_heads))
        value_grads.append(join(dv_heads))
    return (jnp.concatenate(outputs, 0), jnp.concatenate(query_grads, 0), jnp.concatenate(key_grads, 0),
            jnp.concatenate(value_grads, 0), kernel_total)
```

```python
import functools
import math

import jax
import jax.numpy as jnp
from jax import lax
from jax.experimental import pallas as pl
from jax.experimental.pallas import tpu as pltpu
from jax.sharding import Mesh
from jax.sharding import PartitionSpec as P

F32 = jnp.float32
BF = jnp.bfloat16
HD = 96
FD = 128
NB = 8
ROWS = 1024
HALO = 32
TAPS = 31
SCALE = HD**-0.5
LOG2E = math.log2(math.e)
FLOOR = -1e30

VM = pl.BlockSpec(memory_space=pltpu.VMEM)
SM = pl.BlockSpec(memory_space=pltpu.SMEM)


def params():
    return pltpu.CompilerParams(vmem_limit_bytes=48 * 2**20)


def call(body, name, outs, in_specs, scratch=(), out_specs=None, flops=0):
    return pl.pallas_call(
        body,
        name=name,
        out_shape=outs,
        in_specs=in_specs,
        out_specs=out_specs if out_specs is not None else [VM] * len(outs),
        scratch_shapes=list(scratch),
        compiler_params=params(),
        cost_estimate=pl.CostEstimate(flops=flops, bytes_accessed=4 * 2**20, transcendentals=0),
    )


def sds(shape, dtype):
    return jax.ShapeDtypeStruct(shape, dtype)


def dot(a, b):
    return jnp.dot(a, b, preferred_element_type=F32)


def lanes(shape):
    return lax.broadcasted_iota(jnp.int32, shape, len(shape) - 1)


def split3(x):
    a = x.astype(BF)
    r = x - a.astype(F32)
    b = r.astype(BF)
    return a, b, (r - b.astype(F32)).astype(BF)


def pack_body(q, g, k, v, out):
    for n, ref in enumerate((q, g, k, v)):
        t = ref[...].T
        for h in range(NB):
            out[h, n * HD : (n + 1) * HD, :] = t[h * HD : (h + 1) * HD, :]


def prep_body(lengths, zi, r, qa, cot, kv, first, last, flags):
    z = zi[0]
    ends = []
    total = jnp.int32(0)
    for i in range(NB):
        total = total + lengths[0, i]
        ends.append(total)

    def seg(b):
        s = jnp.int32(0)
        for e in ends:
            s = s + (b * ROWS >= e).astype(jnp.int32)
        return s

    own = seg(z)
    for d in range(1, 5):
        flags[d] = (seg((z + NB - d) % NB) == own).astype(jnp.int32)
        flags[8 + d] = (seg((z + d) % NB) == own).astype(jnp.int32)
    flags[0] = jnp.where(z > 0, flags[1], 0)
    flags[8] = jnp.where(z < NB - 1, flags[9], 0)
    for i in (5, 6, 7, 13, 14, 15):
        flags[i] = jnp.int32(0)
    pad = jnp.zeros((FD - HD, FD), BF)
    for s in range(NB):
        rows = slice(s * FD, (s + 1) * FD)
        kv[:, rows] = r[s, 2 * HD : 4 * HD, :]
        q = jnp.concatenate([r[s, 0:HD, :], pad], axis=0).T.astype(F32) * (SCALE * LOG2E)
        hi = q.astype(BF)
        qa[rows, 0:FD] = hi
        qa[rows, FD : 2 * FD] = (q - hi.astype(F32)).astype(BF)
        cot[rows, :] = jnp.concatenate([r[s, HD : 2 * HD, :], pad], axis=0).T
    for ref, rows in ((first, slice(0, HALO)), (last, slice(ROWS - HALO, ROWS))):
        ref[:, 0 : 2 * FD] = qa[rows, :]
        ref[:, 2 * FD : 3 * FD] = cot[rows, :]


def load_keys(k, v, ka, va):
    zero = jnp.zeros((FD - HD, ROWS), BF)
    ka[0:HD, :] = k
    ka[HD:FD, :] = zero
    ka[FD : FD + HD, :] = k
    ka[FD + HD :, :] = zero
    one = (lax.broadcasted_iota(jnp.int32, (FD - HD, ROWS), 0) == 0).astype(F32).astype(BF)
    va[...] = jnp.concatenate([v, one], axis=0).T


def absorb(q, ac, ka, va, kc=512):
    peak = ac[:, HD + 1 : HD + 2]
    for c in range(0, ROWS, kc):
        s = dot(q, ka[:, c : c + kc])
        top = jnp.maximum(peak, jnp.max(s, axis=1, keepdims=True))
        p = jnp.exp2(s - top).astype(BF)
        ac = ac * jnp.exp2(peak - top) + dot(p, va[c : c + kc, :])
        peak = top
    return jnp.where(lanes(ac.shape) == HD + 1, peak, ac)


def empty_rows(rows):
    return jnp.where(lanes((rows, FD)) == HD + 1, FLOOR, 0.0).astype(F32)


def own_body(qa, kv, acc, ka, va):
    load_keys(kv[0:HD, :], kv[HD : 2 * HD, :], ka, va)
    acc[0:ROWS, :] = absorb(qa[...], empty_rows(ROWS), ka, va)
    acc[ROWS:, :] = empty_rows(2 * HALO)


def all_queries(qa, left, right, qs):
    qs[0:ROWS, :] = qa[...]
    qs[ROWS : ROWS + HALO, :] = left[:, 0 : 2 * FD]
    qs[ROWS + HALO :, :] = right[:, 0 : 2 * FD]


def pair_body(step, flags, qa, left, right, kvl, kvr, acc_in, acc, ka, va, qs):
    all_queries(qa, left, right, qs)
    acc[...] = acc_in[...]
    for kv, flag in ((kvl, flags[step]), (kvr, flags[8 + step])):

        @pl.when(flag != 0)
        def _():
            load_keys(kv[0:HD, :], kv[HD : 2 * HD, :], ka, va)
            acc[...] = absorb(qs[...], acc[...], ka, va)


CH = 88
CO = 64


def mid_body(
    flags, qa, left, right, kf, vf, kv, cot, taps, acc_in,
    out_t, kg, qb, qbt, gb, gbt,
    ka, va, qs, acc, cp, cg, ct, tp,
):
    all_queries(qa, left, right, qs)
    acc[...] = acc_in[...]

    @pl.when(flags[4] != 0)
    def _():
        load_keys(kf[...], vf[...], ka, va)
        acc[...] = absorb(qs[...], acc[...], ka, va)

    load_keys(kv[0:HD, :], kv[HD : 2 * HD, :], ka, va)
    acc[ROWS:, :] = absorb(qs[ROWS:, :], acc[ROWS:, :], ka, va)

    a = acc[...]
    weight = a[:, HD : HD + 1]
    ctx = (a / weight).astype(BF).astype(F32)
    ctx = jnp.where(lanes(ctx.shape) < HD, ctx, 0.0)
    lse = a[0:ROWS, HD + 1 : HD + 2] + jnp.log2(weight[0:ROWS])
    keep_l = flags[0] != 0
    keep_r = flags[8] != 0
    cp[0:HALO, :] = jnp.where(keep_l, ctx[ROWS : ROWS + HALO], 0.0)
    cp[HALO : HALO + ROWS, :] = ctx[0:ROWS]
    cp[HALO + ROWS :, :] = jnp.where(keep_r, ctx[ROWS + HALO :], 0.0)
    half = HALO // 2
    cl = left[:, 2 * FD : 3 * FD].astype(F32)
    cr = right[:, 2 * FD : 3 * FD].astype(F32)
    ct[0:half, :] = jnp.where(keep_l, cl[half:], 0.0)
    ct[half : half + ROWS, :] = cot[...].astype(F32)
    ct[half + ROWS :, :] = jnp.where(keep_r, cr[:half], 0.0)
    tp[...] = taps[...]

    ql = lanes((ROWS, FD))
    l1, l2, l3 = split3(-lse)
    hi = jnp.where(ql == HD, l1, jnp.where(ql == HD + 1, l2, jnp.where(ql == HD + 2, l3, qa[:, 0:FD])))
    qb[:, 0:FD] = hi
    qb[:, FD : 2 * FD] = qa[:, FD : 2 * FD]
    qbt[...] = qb[...].T

    def conv_step(i, _):
        base = pl.multiple_of(i * CH, 8)
        conv = jnp.zeros((CH, FD), F32)
        for j in range(TAPS):
            conv = conv + tp[j : j + 1, :] * cp[pl.ds(base + 1 + j, CH), :]
        sig = jax.nn.sigmoid(conv)
        cg[pl.ds(base, CH), :] = ct[pl.ds(base, CH), :] * sig * (1.0 + conv * (1.0 - sig))
        acc[pl.ds(base, CH), :] = conv * sig
        return 0

    lax.fori_loop(0, (ROWS + HALO) // CH, conv_step, 0)
    res = (cp[HALO : HALO + ROWS, :] + acc[half : half + ROWS, :]).astype(BF)
    out_t[...] = res.T[0:HD, :]

    def grad_step(i, totals):
        base = pl.multiple_of(i * CO, 8)
        g = cg[pl.ds(base + half, CO), :]
        new = []
        grad = ct[pl.ds(base + half, CO), :]
        for j in range(TAPS):
            t = g * cp[pl.ds(base + 17 + j, CO), :]
            new.append(totals[j] + jnp.sum(t.reshape(CO // 8, 8, FD), axis=0))
            grad = grad + tp[j : j + 1, :] * cg[pl.ds(base + 31 - j, CO), :]
        low = grad.astype(BF)
        lowf = low.astype(F32)
        delta = jnp.sum(lowf * cp[pl.ds(base + HALO, CO), :], axis=1, keepdims=True)
        d1, d2, d3 = split3(-delta)
        gl = lanes((CO, FD))
        gb[pl.ds(base, CO), :] = jnp.where(
            gl == HD, d1, jnp.where(gl == HD + 1, d2, jnp.where(gl == HD + 2, d3, low))
        )
        return tuple(new)

    zero = jnp.zeros((8, FD), F32)
    totals = lax.fori_loop(0, ROWS // CO, grad_step, (zero,) * TAPS)
    gbt[...] = gb[...].T
    for j in range(TAPS):
        kg[j : j + 1, :] = jnp.sum(totals[j], axis=0, keepdims=True)
    kg[TAPS:, :] = jnp.zeros((1, FD), F32)


def back_block(k, v, qb, qbt, gb, gbt, dq, kn, vn):
    ones = jnp.ones((FD - HD, ROWS), BF)
    kk = jnp.concatenate([k, ones], axis=0).T
    kn[:, 0:FD] = kk
    kn[:, FD : 2 * FD] = kk
    vn[...] = jnp.concatenate([v, ones], axis=0).T
    p = jnp.exp2(dot(kn[...], qbt[...]))
    ds = (p * dot(vn[...], gbt[...])).astype(BF)
    dv = dot(p.astype(BF), gb[...])
    dk = dot(ds, qb[...])
    dq[...] += dot(k, ds)
    dk = (dk[:, 0:FD] + dk[:, FD : 2 * FD]) * (1.0 / LOG2E)
    return dk.T[0:HD, :], dv.T[0:HD, :]


def far_body(flags, qb, qbt, gb, gbt, kf, vf, dq, dk, dv, kn, vn):
    dq[...] = jnp.zeros_like(dq)

    @pl.when(flags[4] == 0)
    def _():
        dk[...] = jnp.zeros_like(dk)
        dv[...] = jnp.zeros_like(dv)

    @pl.when(flags[4] != 0)
    def _():
        a, b = back_block(kf[...], vf[...], qb, qbt, gb, gbt, dq, kn, vn)
        dk[...] = a.astype(BF)
        dv[...] = b.astype(BF)


def back_pair_body(step, flags, qb, qbt, gb, gbt, kvl, kvr, dq_in, dq, dl, dr, kn, vn):
    dq[...] = dq_in[...]
    for kv, out, flag in ((kvl, dl, flags[step]), (kvr, dr, flags[8 + step])):

        @pl.when(flag == 0)
        def _():
            out[...] = jnp.zeros_like(out)

        @pl.when(flag != 0)
        def _():
            a, b = back_block(kv[0:HD, :], kv[HD : 2 * HD, :], qb, qbt, gb, gbt, dq, kn, vn)
            out[0:HD, :] = a.astype(BF)
            out[HD : 2 * HD, :] = b.astype(BF)


def back_own_body(qb, qbt, gb, gbt, kv, dq_in, dqt, dkv, dq, kn, vn):
    dq[...] = dq_in[...]
    a, b = back_block(kv[0:HD, :], kv[HD : 2 * HD, :], qb, qbt, gb, gbt, dq, kn, vn)
    dqt[...] = (dq[...] * SCALE).astype(BF)
    dkv[0:HD, :] = a
    dkv[HD : 2 * HD, :] = b


KG_ROWS = 96


def send_body(out_t, dqt, dkv, rl, rr, kg, out):
    d = (dkv[...] + rl[...].astype(F32) + rr[...].astype(F32)).astype(BF)
    a, b, c = split3(kg[...])
    for s in range(NB):
        rows = slice(s * FD, (s + 1) * FD)
        out[s, 0:HD, :] = out_t[:, rows]
        out[s, HD : 2 * HD, :] = dqt[:, rows]
        out[s, 2 * HD : 4 * HD, :] = d[:, rows]
        out[s, 4 * HD : 4 * HD + 32, :] = a
        out[s, 4 * HD + 32 : 4 * HD + 64, :] = b
        out[s, 4 * HD + 64 : 4 * HD + 96, :] = c


def done_body(r, out, dq, dk, dv, kg):
    for n, ref in enumerate((out, dq, dk, dv)):
        t = jnp.concatenate([r[h, n * HD : (n + 1) * HD, :] for h in range(NB)], axis=0)
        ref[...] = t.T
    for h in range(NB):
        parts = [r[h, 4 * HD + 32 * i : 4 * HD + 32 * (i + 1), :].astype(F32) for i in range(3)]
        whole = (parts[0] + parts[1]) + parts[2]
        kg[:, h * HD : (h + 1) * HD] = whole[0:TAPS, 0:HD]


def shift(a, axis, by):
    n = lax.axis_size(axis)
    return lax.ppermute(a, axis, [(i, (i + by) % n) for i in range(n)])


def add(a, b):
    return (a.astype(F32) + b.astype(F32)).astype(BF)


def local(query, key_in, value, lengths, kernel, cotangent):
    z = lax.axis_index("z").astype(jnp.int32).reshape(1)
    taps = jnp.pad(kernel.astype(F32).reshape(TAPS, NB, HD), ((0, 1), (0, 0), (0, FD - HD)))
    head = lax.axis_index(("x", "c"))
    taps = lax.dynamic_index_in_dim(taps, head, 1, keepdims=False)

    packed = call(pack_body, "pack", [sds((NB, 4 * HD, FD), BF)], [VM] * 4)(
        query, cotangent, key_in, value
    )[0]
    got = lax.all_to_all(packed, ("x", "c"), 0, 0, tiled=True)
    qa, cot, kv, first, last, flags = call(
        prep_body, "prep",
        [sds((ROWS, 2 * FD), BF), sds((ROWS, FD), BF), sds((2 * HD, ROWS), BF),
         sds((HALO, 3 * FD), BF), sds((HALO, 3 * FD), BF), sds((16,), jnp.int32)],
        [SM, SM, VM], out_specs=[VM] * 5 + [SM],
    )(lengths, z, got)

    kvl, kvr = [shift(kv, "z", 1)], [shift(kv, "z", -1)]
    left, right = shift(last, "z", 1), shift(first, "z", -1)
    keys = (pltpu.VMEM((2 * FD, ROWS), BF), pltpu.VMEM((ROWS, FD), BF))
    queries = pltpu.VMEM((ROWS + 2 * HALO, 2 * FD), BF)
    unit = 2 * ROWS * ROWS * 256
    acc_t = sds((ROWS + 2 * HALO, FD), F32)
    acc = call(own_body, "attend_own", [acc_t], [VM] * 2, keys, flops=2 * unit)(qa, kv)[0]
    for step in (1, 2, 3):
        if step < 3:
            kvl.append(shift(kvl[-1], "z", 1))
            kvr.append(shift(kvr[-1], "z", -1))
        else:
            kf = shift(kvl[-1][0:HD], "z", 1)
            vf = shift(kvr[-1][HD:], "z", -1)
        acc = call(
            functools.partial(pair_body, step), f"attend_{step}", [acc_t],
            [SM] + [VM] * 6, keys + (queries,), flops=4 * unit,
        )(flags, qa, left, right, kvl[step - 1], kvr[step - 1], acc)[0]

    wide = ROWS + 2 * HALO
    out_t, kg, qb, qbt, gb, gbt = call(
        mid_body, "middle",
        [sds((HD, ROWS), BF), sds((32, FD), F32), sds((ROWS, 2 * FD), BF), sds((2 * FD, ROWS), BF),
         sds((ROWS, FD), BF), sds((FD, ROWS), BF)],
        [SM] + [VM] * 9,
        keys + (queries, pltpu.VMEM((wide, FD), F32), pltpu.VMEM((wide, FD), F32),
                pltpu.VMEM((wide, FD), F32), pltpu.VMEM((ROWS + HALO, FD), F32), pltpu.VMEM((32, FD), F32)),
        flops=3 * unit,
    )(flags, qa, left, right, kf, vf, kv, cot, taps, acc)

    kg = kg + (shift(kg, "grp", 1) + shift(kg, "grp", 3)) + shift(kg, "grp", 2)
    for by in (1, 2, 4):
        kg = kg + lax.ppermute(kg, "z", [(i, i ^ by) for i in range(NB)])

    back = (pltpu.VMEM((ROWS, 2 * FD), BF), pltpu.VMEM((ROWS, FD), BF))
    ops = (qb, qbt, gb, gbt)
    dq_t = sds((HD, ROWS), F32)
    half_t = sds((HD, ROWS), BF)
    block_t = sds((2 * HD, ROWS), BF)
    dq, dk, dv = call(
        far_body, "back_far", [dq_t, half_t, half_t], [SM] + [VM] * 6, back, flops=5 * unit
    )(flags, *ops, kf, vf)
    rl, rr = shift(dk, "z", 1), shift(dv, "z", -1)
    for step in (3, 2, 1):
        dq, dl, dr = call(
            functools.partial(back_pair_body, step), f"back_{step}", [dq_t, block_t, block_t],
            [SM] + [VM] * 7, back, flops=10 * unit,
        )(flags, *ops, kvl[step - 1], kvr[step - 1], dq)
        if step == 3:
            dr = jnp.concatenate([add(dr[0:HD], rl), dr[HD:]])
            dl = jnp.concatenate([dl[0:HD], add(dl[HD:], rr)])
        else:
            dr, dl = add(dr, rl), add(dl, rr)
        rl, rr = shift(dr, "z", 1), shift(dl, "z", -1)
    dqt, dkv = call(
        back_own_body, "back_own", [half_t, sds((2 * HD, ROWS), F32)], [VM] * 6,
        (pltpu.VMEM((HD, ROWS), F32),) + back, flops=5 * unit,
    )(*ops, kv, dq)
    packed = call(send_body, "pack_out", [sds((NB, 4 * HD + KG_ROWS, FD), BF)], [VM] * 6)(
        out_t, dqt, dkv, rl, rr, kg
    )[0]
    got = lax.all_to_all(packed, ("x", "c"), 0, 0, tiled=True)
    frames = sds((FD, NB * HD), BF)
    outs = [frames] * 4 + [sds((TAPS, NB * HD), F32)]
    return tuple(call(done_body, "unpack_out", outs, [VM])(got))


def solution(mesh):
    fine = Mesh(mesh.devices.reshape(4, 8, 4, 2), ("grp", "z", "x", "c"))
    frames = P(("grp", "z", "x", "c"), None)
    return jax.shard_map(
        local,
        mesh=fine,
        in_specs=(frames, frames, frames, P("grp", None), P(), frames),
        out_specs=(frames, frames, frames, frames, P()),
        check_vma=False,
    )
```

```python
import functools
import math

import jax
import jax.numpy as jnp
from jax import lax
from jax.experimental import pallas as pl
from jax.experimental.pallas import tpu as pltpu
from jax.sharding import Mesh
from jax.sharding import PartitionSpec as P

F32 = jnp.float32
BF = jnp.bfloat16
HD = 96
FD = 128
NB = 8
ROWS = 1024
HALO = 32
EXTRA = 16
TAPS = 31
SCALE = HD**-0.5
LOG2E = math.log2(math.e)
FLOOR = -1e30

VM = pl.BlockSpec(memory_space=pltpu.VMEM)
SM = pl.BlockSpec(memory_space=pltpu.SMEM)


def params(mib):
    return pltpu.CompilerParams(vmem_limit_bytes=mib * 2**20)


def call(body, name, outs, in_specs, scratch=(), out_specs=None, flops=0, mib=16):
    return pl.pallas_call(
        body,
        name=name,
        out_shape=outs,
        in_specs=in_specs,
        out_specs=out_specs if out_specs is not None else [VM] * len(outs),
        scratch_shapes=list(scratch),
        compiler_params=params(mib),
        cost_estimate=pl.CostEstimate(flops=flops, bytes_accessed=4 * 2**20, transcendentals=0),
    )


def sds(shape, dtype):
    return jax.ShapeDtypeStruct(shape, dtype)


def dot(a, b):
    return jnp.dot(a, b, preferred_element_type=F32)


def lanes(shape):
    return lax.broadcasted_iota(jnp.int32, shape, len(shape) - 1)


def split3(x):
    a = x.astype(BF)
    r = x - a.astype(F32)
    b = r.astype(BF)
    return a, b, (r - b.astype(F32)).astype(BF)


def pack_body(head, q, g, k, v, kernel, out, taps, buf, kbuf, sem):
    copies = [pltpu.make_async_copy(ref, buf.at[n], sem.at[n]) for n, ref in enumerate((q, g, k, v))]
    copies.append(pltpu.make_async_copy(kernel, kbuf, sem.at[4]))
    for copy in copies:
        copy.start()
    for n, copy in enumerate(copies):
        copy.wait()
        if n == 4:
            break
        t = buf[n].T
        for h in range(NB):
            out[h, n * HD : (n + 1) * HD, :] = t[h * HD : (h + 1) * HD, :]
    taps[...] = jnp.zeros_like(taps)
    for h in range(NB):

        @pl.when(head[0] == h)
        def _():
            taps[0:TAPS, 0:HD] = kbuf[...].astype(F32)[:, h * HD : (h + 1) * HD]


def prep_body(lengths, zi, r, qa, cot, to_right, to_left, flags):
    z = zi[0]
    ends = []
    total = jnp.int32(0)
    for i in range(NB):
        total = total + lengths[0, i]
        ends.append(total)

    def seg(b):
        s = jnp.int32(0)
        for e in ends:
            s = s + (b * ROWS >= e).astype(jnp.int32)
        return s

    own = seg(z)
    for d in range(1, 5):
        flags[d] = (seg((z + NB - d) % NB) == own).astype(jnp.int32)
        flags[8 + d] = (seg((z + d) % NB) == own).astype(jnp.int32)
    flags[0] = jnp.where(z > 0, flags[1], 0)
    flags[8] = jnp.where(z < NB - 1, flags[9], 0)
    for i in (5, 6, 7, 13, 14, 15):
        flags[i] = jnp.int32(0)
    pad = jnp.zeros((FD - HD, FD), BF)
    for s in range(NB):
        rows = slice(s * FD, (s + 1) * FD)
        to_right[0 : 2 * HD, rows] = r[s, 2 * HD : 4 * HD, :]
        to_left[0 : 2 * HD, rows] = r[s, 2 * HD : 4 * HD, :]
        q = jnp.concatenate([r[s, 0:HD, :], pad], axis=0).T.astype(F32) * (SCALE * LOG2E)
        hi = q.astype(BF)
        qa[rows, 0:FD] = hi
        qa[rows, FD : 2 * FD] = (q - hi.astype(F32)).astype(BF)
        cot[rows, :] = jnp.concatenate([r[s, HD : 2 * HD, :], pad], axis=0).T
    for ref, at in ((to_left, 0), (to_right, ROWS - HALO)):
        for i in range(2):
            rows = slice(at + i * EXTRA, at + (i + 1) * EXTRA)
            ref[2 * HD :, i * FD : (i + 1) * FD] = qa[rows, 0:FD]
            ref[2 * HD :, (2 + i) * FD : (3 + i) * FD] = qa[rows, FD : 2 * FD]
            ref[2 * HD :, (4 + i) * FD : (5 + i) * FD] = cot[rows, :]
        ref[2 * HD :, 6 * FD :] = jnp.zeros((EXTRA, 2 * FD), BF)


def load_keys(k, v, ka, va):
    zero = jnp.zeros((FD - HD, ROWS), BF)
    ka[0:HD, :] = k
    ka[HD:FD, :] = zero
    ka[FD : FD + HD, :] = k
    ka[FD + HD :, :] = zero
    one = (lax.broadcasted_iota(jnp.int32, (FD - HD, ROWS), 0) == 0).astype(F32).astype(BF)
    va[...] = jnp.concatenate([v, one], axis=0).T


def absorb(q, ac, ka, va):
    peak = ac[:, HD + 1 : HD + 2]
    s = dot(q, ka[...])
    top = jnp.maximum(peak, jnp.max(s, axis=1, keepdims=True))
    p = jnp.exp2(s - top).astype(BF)
    ac = ac * jnp.exp2(peak - top) + dot(p, va[...])
    return jnp.where(lanes(ac.shape) == HD + 1, top, ac)


def absorb_all(qs, acc, ka, va):
    for a, b in ((0, ROWS // 2), (ROWS // 2, ROWS + 2 * HALO)):
        acc[a:b, :] = absorb(qs[a:b, :], acc[a:b, :], ka, va)


def empty_rows(rows):
    return jnp.where(lanes((rows, FD)) == HD + 1, FLOOR, 0.0).astype(F32)


def own_body(qa, kv, acc, ka, va):
    load_keys(kv[0:HD, :], kv[HD : 2 * HD, :], ka, va)
    half = ROWS // 2
    for a in (0, half):
        acc[a : a + half, :] = absorb(qa[a : a + half, :], empty_rows(half), ka, va)
    acc[ROWS:, :] = empty_rows(2 * HALO)


def all_queries(qa, left, right, qs):
    qs[0:ROWS, :] = qa[...]
    for n, ref in enumerate((left, right)):
        for i in range(2):
            at = ROWS + n * HALO + i * EXTRA
            qs[at : at + EXTRA, 0:FD] = ref[2 * HD :, i * FD : (i + 1) * FD]
            qs[at : at + EXTRA, FD : 2 * FD] = ref[2 * HD :, (2 + i) * FD : (3 + i) * FD]


def pair_body(step, flags, qa, left, right, kvl, kvr, acc_in, acc, ka, va, qs):
    all_queries(qa, left, right, qs)
    acc[...] = acc_in[...]
    for kv, flag in ((kvl, flags[step]), (kvr, flags[8 + step])):

        @pl.when(flag != 0)
        def _():
            load_keys(kv[0:HD, :], kv[HD : 2 * HD, :], ka, va)
            absorb_all(qs, acc, ka, va)


CH = 88
CO = 64


def mid_body(
    flags, qa, left, right, kf, vf, kv, cot, taps, acc_in,
    out_t, kg, qb, qbt, gb, gbt,
    ka, va, qs, acc, cp, cg, ct, tp,
):
    all_queries(qa, left, right, qs)
    acc[...] = acc_in[...]

    @pl.when(flags[4] != 0)
    def _():
        load_keys(kf[...], vf[...], ka, va)
        absorb_all(qs, acc, ka, va)

    load_keys(kv[0:HD, :], kv[HD : 2 * HD, :], ka, va)
    acc[ROWS:, :] = absorb(qs[ROWS:, :], acc[ROWS:, :], ka, va)

    a = acc[...]
    weight = a[:, HD : HD + 1]
    ctx = (a / weight).astype(BF).astype(F32)
    ctx = jnp.where(lanes(ctx.shape) < HD, ctx, 0.0)
    lse = a[0:ROWS, HD + 1 : HD + 2] + jnp.log2(weight[0:ROWS])
    keep_l = flags[0] != 0
    keep_r = flags[8] != 0
    cp[0:HALO, :] = jnp.where(keep_l, ctx[ROWS : ROWS + HALO], 0.0)
    cp[HALO : HALO + ROWS, :] = ctx[0:ROWS]
    cp[HALO + ROWS :, :] = jnp.where(keep_r, ctx[ROWS + HALO :], 0.0)
    half = HALO // 2
    cl = left[2 * HD :, 5 * FD : 6 * FD].astype(F32)
    cr = right[2 * HD :, 4 * FD : 5 * FD].astype(F32)
    ct[0:half, :] = jnp.where(keep_l, cl, 0.0)
    ct[half : half + ROWS, :] = cot[...].astype(F32)
    ct[half + ROWS :, :] = jnp.where(keep_r, cr, 0.0)
    tp[...] = taps[...]

    ql = lanes((ROWS, FD))
    l1, l2, l3 = split3(-lse)
    hi = jnp.where(ql == HD, l1, jnp.where(ql == HD + 1, l2, jnp.where(ql == HD + 2, l3, qa[:, 0:FD])))
    qb[:, 0:FD] = hi
    qb[:, FD : 2 * FD] = qa[:, FD : 2 * FD]
    qbt[...] = qb[...].T

    def conv_step(i, _):
        base = pl.multiple_of(i * CH, 8)
        conv = jnp.zeros((CH, FD), F32)
        for j in range(TAPS):
            conv = conv + tp[j : j + 1, :] * cp[pl.ds(base + 1 + j, CH), :]
        sig = jax.nn.sigmoid(conv)
        cg[pl.ds(base, CH), :] = ct[pl.ds(base, CH), :] * sig * (1.0 + conv * (1.0 - sig))
        acc[pl.ds(base, CH), :] = conv * sig
        return 0

    lax.fori_loop(0, (ROWS + HALO) // CH, conv_step, 0)
    res = (cp[HALO : HALO + ROWS, :] + acc[half : half + ROWS, :]).astype(BF)
    out_t[...] = res.T[0:HD, :]

    def grad_step(i, totals):
        base = pl.multiple_of(i * CO, 8)
        g = cg[pl.ds(base + half, CO), :]
        new = []
        grad = ct[pl.ds(base + half, CO), :]
        for j in range(TAPS):
            t = g * cp[pl.ds(base + 17 + j, CO), :]
            new.append(totals[j] + jnp.sum(t.reshape(CO // 8, 8, FD), axis=0))
            grad = grad + tp[j : j + 1, :] * cg[pl.ds(base + 31 - j, CO), :]
        low = grad.astype(BF)
        lowf = low.astype(F32)
        delta = jnp.sum(lowf * cp[pl.ds(base + HALO, CO), :], axis=1, keepdims=True)
        d1, d2, d3 = split3(-delta)
        gl = lanes((CO, FD))
        gb[pl.ds(base, CO), :] = jnp.where(
            gl == HD, d1, jnp.where(gl == HD + 1, d2, jnp.where(gl == HD + 2, d3, low))
        )
        return tuple(new)

    zero = jnp.zeros((8, FD), F32)
    totals = lax.fori_loop(0, ROWS // CO, grad_step, (zero,) * TAPS)
    gbt[...] = gb[...].T
    for j in range(TAPS):
        kg[j : j + 1, :] = jnp.sum(totals[j], axis=0, keepdims=True)
    kg[TAPS:, :] = jnp.zeros((1, FD), F32)


def back_block(k, v, qb, qbt, gb, gbt, dq, kn, vn):
    ones = jnp.ones((FD - HD, ROWS), BF)
    kk = jnp.concatenate([k, ones], axis=0).T
    kn[:, 0:FD] = kk
    kn[:, FD : 2 * FD] = kk
    vn[...] = jnp.concatenate([v, ones], axis=0).T
    p = jnp.exp2(dot(kn[...], qbt[...]))
    ds = (p * dot(vn[...], gbt[...])).astype(BF)
    dv = dot(p.astype(BF), gb[...])
    dk = dot(ds, qb[...])
    dq[...] += dot(k, ds)
    dk = (dk[:, 0:FD] + dk[:, FD : 2 * FD]) * (1.0 / LOG2E)
    return dk.T[0:HD, :], dv.T[0:HD, :]


def far_body(flags, qb, qbt, gb, gbt, kf, vf, dq, dk, dv, kn, vn):
    dq[...] = jnp.zeros_like(dq)

    @pl.when(flags[4] == 0)
    def _():
        dk[...] = jnp.zeros_like(dk)
        dv[...] = jnp.zeros_like(dv)

    @pl.when(flags[4] != 0)
    def _():
        a, b = back_block(kf[...], vf[...], qb, qbt, gb, gbt, dq, kn, vn)
        dk[...] = a.astype(BF)
        dv[...] = b.astype(BF)


def back_pair_body(step, flags, qb, qbt, gb, gbt, kvl, kvr, dq_in, dq, dl, dr, kn, vn):
    dq[...] = dq_in[...]
    for kv, out, flag in ((kvl, dl, flags[step]), (kvr, dr, flags[8 + step])):

        @pl.when(flag == 0)
        def _():
            out[...] = jnp.zeros_like(out)

        @pl.when(flag != 0)
        def _():
            a, b = back_block(kv[0:HD, :], kv[HD : 2 * HD, :], qb, qbt, gb, gbt, dq, kn, vn)
            out[0:HD, :] = a.astype(BF)
            out[HD : 2 * HD, :] = b.astype(BF)


def back_own_body(qb, qbt, gb, gbt, kv, dq_in, dqt, dkv, dq, kn, vn):
    dq[...] = dq_in[...]
    a, b = back_block(kv[0:HD, :], kv[HD : 2 * HD, :], qb, qbt, gb, gbt, dq, kn, vn)
    dqt[...] = (dq[...] * SCALE).astype(BF)
    dkv[0:HD, :] = a
    dkv[HD : 2 * HD, :] = b


KG_ROWS = 64


def split2(x):
    a = x.astype(BF)
    return a, (x - a.astype(F32)).astype(BF)


def put_taps(ref, at, x):
    for n, part in enumerate(split2(x)):
        for i in range(2):
            lane = (2 * n + i) * FD
            ref[at : at + EXTRA, lane : lane + FD] = part[i * EXTRA : (i + 1) * EXTRA]
    ref[at : at + EXTRA, 4 * FD :] = jnp.zeros((EXTRA, 4 * FD), BF)


def get_taps(ref, at):
    p = [ref[at : at + EXTRA, i * FD : (i + 1) * FD].astype(F32) for i in range(4)]
    return jnp.concatenate([p[0] + p[2], p[1] + p[3]], axis=0)


def first_body(yi, dk, dv, k0, k1, k2, k3, to_right, to_left, slots):
    y = yi[0]
    for i, ref in enumerate((k0, k1, k2, k3)):
        slots[(y + 4 - i) % 4] = ref[...]
    total = ((slots[0] + slots[1]) + slots[2]) + slots[3]
    to_right[0:HD, :] = dk[...]
    to_left[0:HD, :] = dv[...]
    put_taps(to_right, HD, total)
    to_left[HD:, :] = to_right[HD:, :]


def merge_body(dl, dr, rl, rr, to_right, to_left):
    if rl.shape[0] == HD + EXTRA:
        to_right[0:HD, :] = (dr[0:HD, :].astype(F32) + rl[0:HD, :].astype(F32)).astype(BF)
        to_right[HD : 2 * HD, :] = dr[HD:, :]
        to_left[0:HD, :] = dl[0:HD, :]
        to_left[HD : 2 * HD, :] = (dl[HD:, :].astype(F32) + rr[0:HD, :].astype(F32)).astype(BF)
    else:
        for out, own, got in ((to_right, dr, rl), (to_left, dl, rr)):
            out[0 : 2 * HD, :] = (own[...].astype(F32) + got[0 : 2 * HD, :].astype(F32)).astype(BF)
    to_right[2 * HD :, :] = rl[rl.shape[0] - EXTRA :, :]
    to_left[2 * HD :, :] = rr[rr.shape[0] - EXTRA :, :]


def send_body(zi, out_t, dqt, dkv, mine, l1, l2, l3, l4, r1, r2, r3, r4, out, slots):
    z = zi[0]
    slots[z] = get_taps(mine, HD)
    for i, ref in enumerate((l1, l2, l3, l4)):
        slots[(z + NB - 1 - i) % NB] = get_taps(ref, HD if i == 0 else 2 * HD)
    for i, ref in enumerate((r1, r2, r3)):
        slots[(z + 1 + i) % NB] = get_taps(ref, HD if i == 0 else 2 * HD)
    total = slots[0]
    for i in range(1, NB):
        total = total + slots[i]
    a, b = split2(total)
    d = (dkv[...] + l4[0 : 2 * HD, :].astype(F32) + r4[0 : 2 * HD, :].astype(F32)).astype(BF)
    for s in range(NB):
        rows = slice(s * FD, (s + 1) * FD)
        out[s, 0:HD, :] = out_t[:, rows]
        out[s, HD : 2 * HD, :] = dqt[:, rows]
        out[s, 2 * HD : 4 * HD, :] = d[:, rows]
        out[s, 4 * HD : 4 * HD + 32, :] = a
        out[s, 4 * HD + 32 :, :] = b


def done_body(r, out, dq, dk, dv, kg):
    for n, ref in enumerate((out, dq, dk, dv)):
        t = jnp.concatenate([r[h, n * HD : (n + 1) * HD, :] for h in range(NB)], axis=0)
        ref[...] = t.T
    for h in range(NB):
        parts = [r[h, 4 * HD + 32 * i : 4 * HD + 32 * (i + 1), :].astype(F32) for i in range(2)]
        whole = parts[0] + parts[1]
        kg[:, h * HD : (h + 1) * HD] = whole[0:TAPS, 0:HD]


def shift(a, axis, by):
    n = lax.axis_size(axis)
    return lax.ppermute(a, axis, [(i, (i + by) % n) for i in range(n)])


def local(query, key_in, value, lengths, kernel, cotangent):
    z = lax.axis_index("z").astype(jnp.int32).reshape(1)
    head = lax.axis_index(("x", "c")).astype(jnp.int32).reshape(1)
    hbm = pl.BlockSpec(memory_space=pltpu.HBM)
    packed, taps = call(
        pack_body, "pack", [sds((NB, 4 * HD, FD), BF), sds((32, FD), F32)], [SM] + [hbm] * 5,
        (pltpu.VMEM((4, FD, NB * HD), BF), pltpu.VMEM((TAPS, NB * HD), BF),
         pltpu.SemaphoreType.DMA((5,))), mib=60,
    )(head, query, cotangent, key_in, value, kernel)
    got = lax.all_to_all(packed, ("x", "c"), 0, 0, tiled=True)
    block_t = sds((2 * HD, ROWS), BF)
    wide_t = sds((2 * HD + EXTRA, ROWS), BF)
    qa, cot, kv, to_left, flags = call(
        prep_body, "prep",
        [sds((ROWS, 2 * FD), BF), sds((ROWS, FD), BF), wide_t, wide_t, sds((16,), jnp.int32)],
        [SM, SM, VM], out_specs=[VM] * 4 + [SM],
    )(lengths, z, got)

    kvl, kvr = [shift(kv, "z", 1)], [shift(to_left, "z", -1)]
    keys = (pltpu.VMEM((2 * FD, ROWS), BF), pltpu.VMEM((ROWS, FD), BF))
    queries = pltpu.VMEM((ROWS + 2 * HALO, 2 * FD), BF)
    unit = 2 * ROWS * ROWS * 256
    acc_t = sds((ROWS + 2 * HALO, FD), F32)
    acc = call(own_body, "attend_own", [acc_t], [VM] * 2, keys, flops=2 * unit, mib=20)(qa, kv)[0]
    for step in (1, 2, 3):
        acc, kvl[-1], kvr[-1] = lax.optimization_barrier((acc, kvl[-1], kvr[-1]))
        if step < 3:
            kvl.append(shift(kvl[-1], "z", 1))
            kvr.append(shift(kvr[-1], "z", -1))
        else:
            kf = shift(kvl[-1][0:HD], "z", 1)
            vf = shift(kvr[-1][HD : 2 * HD], "z", -1)
        acc = call(
            functools.partial(pair_body, step), f"attend_{step}", [acc_t],
            [SM] + [VM] * 6, keys + (queries,), flops=4 * unit, mib=20,
        )(flags, qa, kvl[0], kvr[0], kvl[step - 1], kvr[step - 1], acc)[0]

    wide = ROWS + 2 * HALO
    out_t, kg, qb, qbt, gb, gbt = call(
        mid_body, "middle",
        [sds((HD, ROWS), BF), sds((32, FD), F32), sds((ROWS, 2 * FD), BF), sds((2 * FD, ROWS), BF),
         sds((ROWS, FD), BF), sds((FD, ROWS), BF)],
        [SM] + [VM] * 9,
        keys + (queries, pltpu.VMEM((wide, FD), F32), pltpu.VMEM((wide, FD), F32),
                pltpu.VMEM((wide, FD), F32), pltpu.VMEM((ROWS + HALO, FD), F32), pltpu.VMEM((32, FD), F32)),
        flops=3 * unit, mib=24,
    )(flags, qa, kvl[0], kvr[0], kf, vf, kv, cot, taps, acc)

    kgs = [kg] + [shift(kg, "grp", i) for i in (1, 2, 3)]
    back = (pltpu.VMEM((ROWS, 2 * FD), BF), pltpu.VMEM((ROWS, FD), BF))
    ops = (qb, qbt, gb, gbt)
    dq_t = sds((HD, ROWS), F32)
    half_t = sds((HD, ROWS), BF)
    dq, dk, dv = call(
        far_body, "back_far", [dq_t, half_t, half_t], [SM] + [VM] * 6, back, flops=5 * unit, mib=32
    )(flags, *ops, kf, vf)
    y = lax.axis_index("grp").astype(jnp.int32).reshape(1)
    far_t = sds((HD + EXTRA, ROWS), BF)
    mine, to_left = call(
        first_body, "first", [far_t, far_t], [SM] + [VM] * 6, (pltpu.VMEM((4, 32, FD), F32),)
    )(y, dk, dv, *kgs)
    rl, rr = [shift(mine, "z", 1)], [shift(to_left, "z", -1)]
    for step in (3, 2, 1):
        dq, dl, dr = call(
            functools.partial(back_pair_body, step), f"back_{step}", [dq_t, block_t, block_t],
            [SM] + [VM] * 7, back, flops=10 * unit, mib=32,
        )(flags, *ops, kvl[step - 1], kvr[step - 1], dq)
        to_right, to_left = call(merge_body, f"merge_{step}", [wide_t, wide_t], [VM] * 4)(
            dl, dr, rl[-1], rr[-1]
        )
        rl.append(shift(to_right, "z", 1))
        rr.append(shift(to_left, "z", -1))
    dqt, dkv = call(
        back_own_body, "back_own", [half_t, sds((2 * HD, ROWS), F32)], [VM] * 6,
        (pltpu.VMEM((HD, ROWS), F32),) + back, flops=5 * unit, mib=32,
    )(*ops, kv, dq)
    packed = call(
        send_body, "pack_out", [sds((NB, 4 * HD + KG_ROWS, FD), BF)], [SM] + [VM] * 12,
        (pltpu.VMEM((NB, 32, FD), F32),),
    )(z, out_t, dqt, dkv, mine, *rl, *rr)[0]
    got = lax.all_to_all(packed, ("x", "c"), 0, 0, tiled=True)
    frames = sds((FD, NB * HD), BF)
    outs = [frames] * 4 + [sds((TAPS, NB * HD), F32)]
    return tuple(call(done_body, "unpack_out", outs, [VM])(got))


def solution(mesh):
    fine = Mesh(mesh.devices.reshape(4, 8, 4, 2), ("grp", "z", "x", "c"))
    frames = P(("grp", "z", "x", "c"), None)
    return jax.shard_map(
        local,
        mesh=fine,
        in_specs=(frames, frames, frames, P("grp", None), P(), frames),
        out_specs=(frames, frames, frames, frames, P()),
        check_vma=False,
    )
```

```python
import functools
import math

import jax
import jax.numpy as jnp
from jax import lax
from jax.experimental import pallas as pl
from jax.experimental.pallas import tpu as pltpu
from jax.sharding import Mesh
from jax.sharding import PartitionSpec as P

F32 = jnp.float32
BF = jnp.bfloat16
HD = 96
FD = 128
NB = 8
ROWS = 1024
HALO = 32
EXTRA = 16
TAPS = 31
SCALE = HD**-0.5
LOG2E = math.log2(math.e)
FLOOR = -1e30

VM = pl.BlockSpec(memory_space=pltpu.VMEM)
SM = pl.BlockSpec(memory_space=pltpu.SMEM)


def params(mib):
    return pltpu.CompilerParams(vmem_limit_bytes=mib * 2**20)


def call(body, name, outs, in_specs, scratch=(), out_specs=None, flops=0, mib=16):
    return pl.pallas_call(
        body,
        name=name,
        out_shape=outs,
        in_specs=in_specs,
        out_specs=out_specs if out_specs is not None else [VM] * len(outs),
        scratch_shapes=list(scratch),
        compiler_params=params(mib),
        cost_estimate=pl.CostEstimate(flops=flops, bytes_accessed=4 * 2**20, transcendentals=0),
    )


def sds(shape, dtype):
    return jax.ShapeDtypeStruct(shape, dtype)


def dot(a, b):
    return jnp.dot(a, b, preferred_element_type=F32)


def lanes(shape):
    return lax.broadcasted_iota(jnp.int32, shape, len(shape) - 1)


def split3(x):
    a = x.astype(BF)
    r = x - a.astype(F32)
    b = r.astype(BF)
    return a, b, (r - b.astype(F32)).astype(BF)


def pack_body(head, q, g, k, v, kernel, out, taps, buf, kbuf, sem):
    copies = [pltpu.make_async_copy(ref, buf.at[n], sem.at[n]) for n, ref in enumerate((q, g, k, v))]
    copies.append(pltpu.make_async_copy(kernel, kbuf, sem.at[4]))
    for copy in copies:
        copy.start()
    for n, copy in enumerate(copies):
        copy.wait()
        if n == 4:
            break
        t = buf[n].T
        for h in range(NB):
            out[h, n * HD : (n + 1) * HD, :] = t[h * HD : (h + 1) * HD, :]
    taps[...] = jnp.zeros_like(taps)
    for h in range(NB):

        @pl.when(head[0] == h)
        def _():
            taps[0:TAPS, 0:HD] = kbuf[...].astype(F32)[:, h * HD : (h + 1) * HD]


def scaled(q):
    pad = jnp.zeros((FD - HD, FD), BF)
    q = jnp.concatenate([q, pad], axis=0).T.astype(F32) * (SCALE * LOG2E)
    hi = q.astype(BF)
    return hi, (q - hi.astype(F32)).astype(BF)


def natural(x):
    return jnp.concatenate([x, jnp.zeros((FD - HD, FD), BF)], axis=0).T


def keys_body(r, to_right, to_left):
    for s in range(NB):
        rows = slice(s * FD, (s + 1) * FD)
        to_right[0 : 2 * HD, rows] = r[s, 2 * HD : 4 * HD, :]
        to_left[0 : 2 * HD, rows] = r[s, 2 * HD : 4 * HD, :]
    for ref, s, at in ((to_left, 0, 0), (to_right, NB - 1, FD - HALO)):
        parts = scaled(r[s, 0:HD, :]) + (natural(r[s, HD : 2 * HD, :]),)
        for n, part in enumerate(parts):
            for i in range(2):
                lane = (2 * n + i) * FD
                ref[2 * HD :, lane : lane + FD] = part[at + i * EXTRA : at + (i + 1) * EXTRA]
        ref[2 * HD :, 6 * FD :] = jnp.zeros((EXTRA, 2 * FD), BF)


def prep_body(lengths, zi, r, qa, cot, flags):
    z = zi[0]
    ends = []
    total = jnp.int32(0)
    for i in range(NB):
        total = total + lengths[0, i]
        ends.append(total)

    def seg(b):
        s = jnp.int32(0)
        for e in ends:
            s = s + (b * ROWS >= e).astype(jnp.int32)
        return s

    own = seg(z)
    for d in range(1, 5):
        flags[d] = (seg((z + NB - d) % NB) == own).astype(jnp.int32)
        flags[8 + d] = (seg((z + d) % NB) == own).astype(jnp.int32)
    flags[0] = jnp.where(z > 0, flags[1], 0)
    flags[8] = jnp.where(z < NB - 1, flags[9], 0)
    for i in (5, 6, 7, 13, 14, 15):
        flags[i] = jnp.int32(0)
    for s in range(NB):
        rows = slice(s * FD, (s + 1) * FD)
        hi, lo = scaled(r[s, 0:HD, :])
        qa[rows, 0:FD] = hi
        qa[rows, FD : 2 * FD] = lo
        cot[rows, :] = natural(r[s, HD : 2 * HD, :])


def load_keys(k, v, ka, va):
    zero = jnp.zeros((FD - HD, ROWS), BF)
    ka[0:HD, :] = k
    ka[HD:FD, :] = zero
    ka[FD : FD + HD, :] = k
    ka[FD + HD :, :] = zero
    one = (lax.broadcasted_iota(jnp.int32, (FD - HD, ROWS), 0) == 0).astype(F32).astype(BF)
    va[...] = jnp.concatenate([v, one], axis=0).T


def absorb(q, ac, ka, va):
    peak = ac[:, HD + 1 : HD + 2]
    s = dot(q, ka[...])
    top = jnp.maximum(peak, jnp.max(s, axis=1, keepdims=True))
    p = jnp.exp2(s - top).astype(BF)
    ac = ac * jnp.exp2(peak - top) + dot(p, va[...])
    return jnp.where(lanes(ac.shape) == HD + 1, top, ac)


def absorb_all(qs, acc, ka, va):
    for a, b in ((0, ROWS // 2), (ROWS // 2, ROWS + 2 * HALO)):
        acc[a:b, :] = absorb(qs[a:b, :], acc[a:b, :], ka, va)


def empty_rows(rows):
    return jnp.where(lanes((rows, FD)) == HD + 1, FLOOR, 0.0).astype(F32)


def own_body(qa, kv, acc, ka, va):
    load_keys(kv[0:HD, :], kv[HD : 2 * HD, :], ka, va)
    half = ROWS // 2
    for a in (0, half):
        acc[a : a + half, :] = absorb(qa[a : a + half, :], empty_rows(half), ka, va)
    acc[ROWS:, :] = empty_rows(2 * HALO)


def all_queries(qa, left, right, qs):
    qs[0:ROWS, :] = qa[...]
    for n, ref in enumerate((left, right)):
        for i in range(2):
            at = ROWS + n * HALO + i * EXTRA
            qs[at : at + EXTRA, 0:FD] = ref[2 * HD :, i * FD : (i + 1) * FD]
            qs[at : at + EXTRA, FD : 2 * FD] = ref[2 * HD :, (2 + i) * FD : (3 + i) * FD]


def pair_body(step, flags, qa, left, right, kvl, kvr, acc_in, *refs):
    own, (acc, ka, va, qs) = refs[:-4], refs[-4:]
    all_queries(qa, left, right, qs)
    acc[...] = acc_in[...]
    if own:
        load_keys(own[0][0:HD, :], own[0][HD : 2 * HD, :], ka, va)
        acc[ROWS:, :] = absorb(qs[ROWS:, :], acc[ROWS:, :], ka, va)
    for kv, flag in ((kvl, flags[step]), (kvr, flags[8 + step])):

        @pl.when(flag != 0)
        def _():
            load_keys(kv[0:HD, :], kv[HD : 2 * HD, :], ka, va)
            absorb_all(qs, acc, ka, va)


CH = 88
CO = 64


def mid_body(
    flags, qa, left, right, kf, vf, cot, taps, acc_in,
    out_t, kg, qb, qbt, gb, gbt,
    ka, va, qs, acc, cp, cg, ct, tp,
):
    all_queries(qa, left, right, qs)
    acc[...] = acc_in[...]

    @pl.when(flags[4] != 0)
    def _():
        load_keys(kf[...], vf[...], ka, va)
        absorb_all(qs, acc, ka, va)

    a = acc[...]
    weight = a[:, HD : HD + 1]
    ctx = (a / weight).astype(BF).astype(F32)
    ctx = jnp.where(lanes(ctx.shape) < HD, ctx, 0.0)
    lse = a[0:ROWS, HD + 1 : HD + 2] + jnp.log2(weight[0:ROWS])
    keep_l = flags[0] != 0
    keep_r = flags[8] != 0
    cp[0:HALO, :] = jnp.where(keep_l, ctx[ROWS : ROWS + HALO], 0.0)
    cp[HALO : HALO + ROWS, :] = ctx[0:ROWS]
    cp[HALO + ROWS :, :] = jnp.where(keep_r, ctx[ROWS + HALO :], 0.0)
    half = HALO // 2
    cl = left[2 * HD :, 5 * FD : 6 * FD].astype(F32)
    cr = right[2 * HD :, 4 * FD : 5 * FD].astype(F32)
    ct[0:half, :] = jnp.where(keep_l, cl, 0.0)
    ct[half : half + ROWS, :] = cot[...].astype(F32)
    ct[half + ROWS :, :] = jnp.where(keep_r, cr, 0.0)
    tp[...] = taps[...]

    ql = lanes((ROWS, FD))
    l1, l2, l3 = split3(-lse)
    hi = jnp.where(ql == HD, l1, jnp.where(ql == HD + 1, l2, jnp.where(ql == HD + 2, l3, qa[:, 0:FD])))
    qb[:, 0:FD] = hi
    qb[:, FD : 2 * FD] = qa[:, FD : 2 * FD]
    qbt[...] = qb[...].T

    def conv_step(i, _):
        base = pl.multiple_of(i * CH, 8)
        conv = jnp.zeros((CH, FD), F32)
        for j in range(TAPS):
            conv = conv + tp[j : j + 1, :] * cp[pl.ds(base + 1 + j, CH), :]
        sig = jax.nn.sigmoid(conv)
        cg[pl.ds(base, CH), :] = ct[pl.ds(base, CH), :] * sig * (1.0 + conv * (1.0 - sig))
        acc[pl.ds(base, CH), :] = conv * sig
        return 0

    lax.fori_loop(0, (ROWS + HALO) // CH, conv_step, 0)
    res = (cp[HALO : HALO + ROWS, :] + acc[half : half + ROWS, :]).astype(BF)
    out_t[...] = res.T[0:HD, :]

    def grad_step(i, totals):
        base = pl.multiple_of(i * CO, 8)
        g = cg[pl.ds(base + half, CO), :]
        new = []
        grad = ct[pl.ds(base + half, CO), :]
        for j in range(TAPS):
            t = g * cp[pl.ds(base + 17 + j, CO), :]
            new.append(totals[j] + jnp.sum(t.reshape(CO // 8, 8, FD), axis=0))
            grad = grad + tp[j : j + 1, :] * cg[pl.ds(base + 31 - j, CO), :]
        low = grad.astype(BF)
        lowf = low.astype(F32)
        delta = jnp.sum(lowf * cp[pl.ds(base + HALO, CO), :], axis=1, keepdims=True)
        d1, d2, d3 = split3(-delta)
        gl = lanes((CO, FD))
        gb[pl.ds(base, CO), :] = jnp.where(
            gl == HD, d1, jnp.where(gl == HD + 1, d2, jnp.where(gl == HD + 2, d3, low))
        )
        return tuple(new)

    zero = jnp.zeros((8, FD), F32)
    totals = lax.fori_loop(0, ROWS // CO, grad_step, (zero,) * TAPS)
    gbt[...] = gb[...].T
    for j in range(TAPS):
        kg[j : j + 1, :] = jnp.sum(totals[j], axis=0, keepdims=True)
    kg[TAPS:, :] = jnp.zeros((1, FD), F32)


def back_block(k, v, qb, qbt, gb, gbt, dq, kn, vn):
    ones = jnp.ones((FD - HD, ROWS), BF)
    kk = jnp.concatenate([k, ones], axis=0).T
    kn[:, 0:FD] = kk
    kn[:, FD : 2 * FD] = kk
    vn[...] = jnp.concatenate([v, ones], axis=0).T
    p = jnp.exp2(dot(kn[...], qbt[...]))
    ds = (p * dot(vn[...], gbt[...])).astype(BF)
    dv = dot(p.astype(BF), gb[...])
    dk = dot(ds, qb[...])
    dq[...] += dot(k, ds)
    dk = (dk[:, 0:FD] + dk[:, FD : 2 * FD]) * (1.0 / LOG2E)
    return dk.T[0:HD, :], dv.T[0:HD, :]


def far_body(flags, qb, qbt, gb, gbt, kf, vf, dq, dk, dv, kn, vn):
    dq[...] = jnp.zeros_like(dq)

    @pl.when(flags[4] == 0)
    def _():
        dk[...] = jnp.zeros_like(dk)
        dv[...] = jnp.zeros_like(dv)

    @pl.when(flags[4] != 0)
    def _():
        a, b = back_block(kf[...], vf[...], qb, qbt, gb, gbt, dq, kn, vn)
        dk[...] = a.astype(BF)
        dv[...] = b.astype(BF)


def back_pair_body(step, flags, qb, qbt, gb, gbt, kvl, kvr, dq_in, dq, dl, dr, kn, vn):
    dq[...] = dq_in[...]
    for kv, out, flag in ((kvl, dl, flags[step]), (kvr, dr, flags[8 + step])):

        @pl.when(flag == 0)
        def _():
            out[...] = jnp.zeros_like(out)

        @pl.when(flag != 0)
        def _():
            a, b = back_block(kv[0:HD, :], kv[HD : 2 * HD, :], qb, qbt, gb, gbt, dq, kn, vn)
            out[0:HD, :] = a.astype(BF)
            out[HD : 2 * HD, :] = b.astype(BF)


def back_own_body(qb, qbt, gb, gbt, kv, dq_in, dqt, dkv, dq, kn, vn):
    dq[...] = dq_in[...]
    a, b = back_block(kv[0:HD, :], kv[HD : 2 * HD, :], qb, qbt, gb, gbt, dq, kn, vn)
    dqt[...] = (dq[...] * SCALE).astype(BF)
    dkv[0:HD, :] = a
    dkv[HD : 2 * HD, :] = b


KG_ROWS = 32


def split2(x):
    a = x.astype(BF)
    return a, (x - a.astype(F32)).astype(BF)


def put_taps(ref, at, x):
    for n, part in enumerate(split2(x)):
        for i in range(2):
            lane = (2 * n + i) * FD
            ref[at : at + EXTRA, lane : lane + FD] = part[i * EXTRA : (i + 1) * EXTRA]
    ref[at : at + EXTRA, 4 * FD :] = jnp.zeros((EXTRA, 4 * FD), BF)


def get_taps(ref, at):
    p = [ref[at : at + EXTRA, i * FD : (i + 1) * FD].astype(F32) for i in range(4)]
    return jnp.concatenate([p[0] + p[2], p[1] + p[3]], axis=0)


def first_body(yi, dk, dv, k0, k1, k2, k3, to_right, to_left, slots):
    y = yi[0]
    for i, ref in enumerate((k0, k1, k2, k3)):
        slots[(y + 4 - i) % 4] = ref[...]
    total = ((slots[0] + slots[1]) + slots[2]) + slots[3]
    to_right[0:HD, :] = dk[...]
    to_left[0:HD, :] = dv[...]
    put_taps(to_right, HD, total)
    to_left[HD:, :] = to_right[HD:, :]


def merge_body(dl, dr, rl, rr, to_right, to_left):
    if rl.shape[0] == HD + EXTRA:
        to_right[0:HD, :] = (dr[0:HD, :].astype(F32) + rl[0:HD, :].astype(F32)).astype(BF)
        to_right[HD : 2 * HD, :] = dr[HD:, :]
        to_left[0:HD, :] = dl[0:HD, :]
        to_left[HD : 2 * HD, :] = (dl[HD:, :].astype(F32) + rr[0:HD, :].astype(F32)).astype(BF)
    else:
        for out, own, got in ((to_right, dr, rl), (to_left, dl, rr)):
            out[0 : 2 * HD, :] = (own[...].astype(F32) + got[0 : 2 * HD, :].astype(F32)).astype(BF)
    to_right[2 * HD :, :] = rl[rl.shape[0] - EXTRA :, :]
    to_left[2 * HD :, :] = rr[rr.shape[0] - EXTRA :, :]


def send_body(zi, out_t, dqt, dkv, mine, l1, l2, l3, l4, r1, r2, r3, r4, out, slots):
    z = zi[0]
    slots[z] = get_taps(mine, HD)
    for i, ref in enumerate((l1, l2, l3, l4)):
        slots[(z + NB - 1 - i) % NB] = get_taps(ref, HD if i == 0 else 2 * HD)
    for i, ref in enumerate((r1, r2, r3)):
        slots[(z + 1 + i) % NB] = get_taps(ref, HD if i == 0 else 2 * HD)
    total = slots[0]
    for i in range(1, NB):
        total = total + slots[i]
    low = total.astype(BF)
    d = (dkv[...] + l4[0 : 2 * HD, :].astype(F32) + r4[0 : 2 * HD, :].astype(F32)).astype(BF)
    for s in range(NB):
        rows = slice(s * FD, (s + 1) * FD)
        out[s, 0:HD, :] = out_t[:, rows]
        out[s, HD : 2 * HD, :] = dqt[:, rows]
        out[s, 2 * HD : 4 * HD, :] = d[:, rows]
        out[s, 4 * HD :, :] = low


def done_body(r, out, dq, dk, dv, kg):
    for n, ref in enumerate((out, dq, dk, dv)):
        t = jnp.concatenate([r[h, n * HD : (n + 1) * HD, :] for h in range(NB)], axis=0)
        ref[...] = t.T
    for h in range(NB):
        whole = r[h, 4 * HD :, :].astype(F32)
        kg[:, h * HD : (h + 1) * HD] = whole[0:TAPS, 0:HD]


def shift(a, axis, by):
    n = lax.axis_size(axis)
    return lax.ppermute(a, axis, [(i, (i + by) % n) for i in range(n)])


def local(query, key_in, value, lengths, kernel, cotangent):
    z = lax.axis_index("z").astype(jnp.int32).reshape(1)
    head = lax.axis_index(("x", "c")).astype(jnp.int32).reshape(1)
    hbm = pl.BlockSpec(memory_space=pltpu.HBM)
    packed, taps = call(
        pack_body, "pack", [sds((NB, 4 * HD, FD), BF), sds((32, FD), F32)], [SM] + [hbm] * 5,
        (pltpu.VMEM((4, FD, NB * HD), BF), pltpu.VMEM((TAPS, NB * HD), BF),
         pltpu.SemaphoreType.DMA((5,))), mib=60,
    )(head, query, cotangent, key_in, value, kernel)
    got = lax.all_to_all(packed, ("x", "c"), 0, 0, tiled=True)
    block_t = sds((2 * HD, ROWS), BF)
    wide_t = sds((2 * HD + EXTRA, ROWS), BF)
    kv, to_left = call(keys_body, "keys", [wide_t, wide_t], [VM])(got)
    kvl, kvr = [shift(kv, "z", 1)], [shift(to_left, "z", -1)]
    qa, cot, flags = call(
        prep_body, "prep", [sds((ROWS, 2 * FD), BF), sds((ROWS, FD), BF), sds((16,), jnp.int32)],
        [SM, SM, VM], out_specs=[VM] * 2 + [SM],
    )(lengths, z, got)
    keys = (pltpu.VMEM((2 * FD, ROWS), BF), pltpu.VMEM((ROWS, FD), BF))
    queries = pltpu.VMEM((ROWS + 2 * HALO, 2 * FD), BF)
    unit = 2 * ROWS * ROWS * 256
    acc_t = sds((ROWS + 2 * HALO, FD), F32)
    acc = call(own_body, "attend_own", [acc_t], [VM] * 2, keys, flops=2 * unit, mib=20)(qa, kv)[0]
    for step in (1, 2, 3):
        acc, kvl[-1], kvr[-1] = lax.optimization_barrier((acc, kvl[-1], kvr[-1]))
        if step < 3:
            kvl.append(shift(kvl[-1], "z", 1))
            kvr.append(shift(kvr[-1], "z", -1))
        else:
            kf = shift(kvl[-1][0:HD], "z", 1)
            vf = shift(kvr[-1][HD : 2 * HD], "z", -1)
        own = (kv,) if step == 1 else ()
        acc = call(
            functools.partial(pair_body, step), f"attend_{step}", [acc_t],
            [SM] + [VM] * (6 + len(own)), keys + (queries,), flops=4 * unit, mib=20,
        )(flags, qa, kvl[0], kvr[0], kvl[step - 1], kvr[step - 1], acc, *own)[0]

    wide = ROWS + 2 * HALO
    out_t, kg, qb, qbt, gb, gbt = call(
        mid_body, "middle",
        [sds((HD, ROWS), BF), sds((32, FD), F32), sds((ROWS, 2 * FD), BF), sds((2 * FD, ROWS), BF),
         sds((ROWS, FD), BF), sds((FD, ROWS), BF)],
        [SM] + [VM] * 8,
        keys + (queries, pltpu.VMEM((wide, FD), F32), pltpu.VMEM((wide, FD), F32),
                pltpu.VMEM((wide, FD), F32), pltpu.VMEM((ROWS + HALO, FD), F32), pltpu.VMEM((32, FD), F32)),
        flops=3 * unit, mib=24,
    )(flags, qa, kvl[0], kvr[0], kf, vf, cot, taps, acc)

    kgs = [kg] + [shift(kg, "grp", i) for i in (1, 2, 3)]
    back = (pltpu.VMEM((ROWS, 2 * FD), BF), pltpu.VMEM((ROWS, FD), BF))
    ops = (qb, qbt, gb, gbt)
    dq_t = sds((HD, ROWS), F32)
    half_t = sds((HD, ROWS), BF)
    dq, dk, dv = call(
        far_body, "back_far", [dq_t, half_t, half_t], [SM] + [VM] * 6, back, flops=5 * unit, mib=32
    )(flags, *ops, kf, vf)
    y = lax.axis_index("grp").astype(jnp.int32).reshape(1)
    far_t = sds((HD + EXTRA, ROWS), BF)
    mine, to_left = call(
        first_body, "first", [far_t, far_t], [SM] + [VM] * 6, (pltpu.VMEM((4, 32, FD), F32),)
    )(y, dk, dv, *kgs)
    rl, rr = [shift(mine, "z", 1)], [shift(to_left, "z", -1)]
    for step in (3, 2, 1):
        dq, dl, dr = call(
            functools.partial(back_pair_body, step), f"back_{step}", [dq_t, block_t, block_t],
            [SM] + [VM] * 7, back, flops=10 * unit, mib=32,
        )(flags, *ops, kvl[step - 1], kvr[step - 1], dq)
        to_right, to_left = call(merge_body, f"merge_{step}", [wide_t, wide_t], [VM] * 4)(
            dl, dr, rl[-1], rr[-1]
        )
        rl.append(shift(to_right, "z", 1))
        rr.append(shift(to_left, "z", -1))
    dqt, dkv = call(
        back_own_body, "back_own", [half_t, sds((2 * HD, ROWS), F32)], [VM] * 6,
        (pltpu.VMEM((HD, ROWS), F32),) + back, flops=5 * unit, mib=32,
    )(*ops, kv, dq)
    packed = call(
        send_body, "pack_out", [sds((NB, 4 * HD + KG_ROWS, FD), BF)], [SM] + [VM] * 12,
        (pltpu.VMEM((NB, 32, FD), F32),),
    )(z, out_t, dqt, dkv, mine, *rl, *rr)[0]
    got = lax.all_to_all(packed, ("x", "c"), 0, 0, tiled=True)
    frames = sds((FD, NB * HD), BF)
    outs = [frames] * 4 + [sds((TAPS, NB * HD), F32)]
    return tuple(call(done_body, "unpack_out", outs, [VM])(got))


def solution(mesh):
    fine = Mesh(mesh.devices.reshape(4, 8, 4, 2), ("grp", "z", "x", "c"))
    frames = P(("grp", "z", "x", "c"), None)
    return jax.shard_map(
        local,
        mesh=fine,
        in_specs=(frames, frames, frames, P("grp", None), P(), frames),
        out_specs=(frames, frames, frames, frames, P()),
        check_vma=False,
    )
```

```python
import functools
import math

import jax
import jax.numpy as jnp
from jax import lax
from jax.experimental import pallas as pl
from jax.experimental.pallas import tpu as pltpu
from jax.sharding import Mesh
from jax.sharding import PartitionSpec as P

F32 = jnp.float32
BF = jnp.bfloat16
HD = 96
FD = 128
NB = 8
ROWS = 1024
HALO = 32
EXTRA = 16
TAPS = 31
SCALE = HD**-0.5
LOG2E = math.log2(math.e)
FLOOR = -1e30

VM = pl.BlockSpec(memory_space=pltpu.VMEM)
SM = pl.BlockSpec(memory_space=pltpu.SMEM)


def params(mib):
    return pltpu.CompilerParams(vmem_limit_bytes=mib * 2**20)


def call(body, name, outs, in_specs, scratch=(), out_specs=None, flops=0, mib=16):
    return pl.pallas_call(
        body,
        name=name,
        out_shape=outs,
        in_specs=in_specs,
        out_specs=out_specs if out_specs is not None else [VM] * len(outs),
        scratch_shapes=list(scratch),
        compiler_params=params(mib),
        cost_estimate=pl.CostEstimate(flops=flops, bytes_accessed=4 * 2**20, transcendentals=0),
    )


def sds(shape, dtype):
    return jax.ShapeDtypeStruct(shape, dtype)


def dot(a, b):
    return jnp.dot(a, b, preferred_element_type=F32)


def lanes(shape):
    return lax.broadcasted_iota(jnp.int32, shape, len(shape) - 1)


def split3(x):
    a = x.astype(BF)
    r = x - a.astype(F32)
    b = r.astype(BF)
    return a, b, (r - b.astype(F32)).astype(BF)


def pack_body(x, out):
    for n in range(4):
        t = x[n].T
        for h in range(NB):
            out[h, n * HD : (n + 1) * HD, :] = t[h * HD : (h + 1) * HD, :]


def scaled(q):
    pad = jnp.zeros((FD - HD, FD), BF)
    q = jnp.concatenate([q, pad], axis=0).T.astype(F32) * (SCALE * LOG2E)
    hi = q.astype(BF)
    return hi, (q - hi.astype(F32)).astype(BF)


def natural(x):
    return jnp.concatenate([x, jnp.zeros((FD - HD, FD), BF)], axis=0).T


def keys_body(r, to_right, to_left):
    for s in range(NB):
        rows = slice(s * FD, (s + 1) * FD)
        to_right[0 : 2 * HD, rows] = r[s, 2 * HD : 4 * HD, :]
        to_left[0 : 2 * HD, rows] = r[s, 2 * HD : 4 * HD, :]
    for ref, s, at in ((to_left, 0, 0), (to_right, NB - 1, FD - HALO)):
        parts = scaled(r[s, 0:HD, :]) + (natural(r[s, HD : 2 * HD, :]),)
        for n, part in enumerate(parts):
            for i in range(2):
                lane = (2 * n + i) * FD
                ref[2 * HD :, lane : lane + FD] = part[at + i * EXTRA : at + (i + 1) * EXTRA]
        ref[2 * HD :, 6 * FD :] = jnp.zeros((EXTRA, 2 * FD), BF)


def prep_body(lengths, zi, head, r, kernel, qa, cot, taps, flags):
    z = zi[0]
    taps[...] = jnp.zeros_like(taps)
    for h in range(NB):

        @pl.when(head[0] == h)
        def _():
            taps[0:TAPS, 0:HD] = kernel[...].astype(F32)[:, h * HD : (h + 1) * HD]

    ends = []
    total = jnp.int32(0)
    for i in range(NB):
        total = total + lengths[0, i]
        ends.append(total)

    def seg(b):
        s = jnp.int32(0)
        for e in ends:
            s = s + (b * ROWS >= e).astype(jnp.int32)
        return s

    own = seg(z)
    for d in range(1, 5):
        flags[d] = (seg((z + NB - d) % NB) == own).astype(jnp.int32)
        flags[8 + d] = (seg((z + d) % NB) == own).astype(jnp.int32)
    flags[0] = jnp.where(z > 0, flags[1], 0)
    flags[8] = jnp.where(z < NB - 1, flags[9], 0)
    for i in (5, 6, 7, 13, 14, 15):
        flags[i] = jnp.int32(0)
    for s in range(NB):
        rows = slice(s * FD, (s + 1) * FD)
        hi, lo = scaled(r[s, 0:HD, :])
        qa[rows, 0:FD] = hi
        qa[rows, FD : 2 * FD] = lo
        cot[rows, :] = natural(r[s, HD : 2 * HD, :])


def load_keys(k, v, ka, va):
    zero = jnp.zeros((FD - HD, ROWS), BF)
    ka[0:HD, :] = k
    ka[HD:FD, :] = zero
    ka[FD : FD + HD, :] = k
    ka[FD + HD :, :] = zero
    one = (lax.broadcasted_iota(jnp.int32, (FD - HD, ROWS), 0) == 0).astype(F32).astype(BF)
    va[...] = jnp.concatenate([v, one], axis=0).T


def absorb(q, ac, ka, va):
    peak = ac[:, HD + 1 : HD + 2]
    s = dot(q, ka[...])
    top = jnp.maximum(peak, jnp.max(s, axis=1, keepdims=True))
    p = jnp.exp2(s - top).astype(BF)
    ac = ac * jnp.exp2(peak - top) + dot(p, va[...])
    return jnp.where(lanes(ac.shape) == HD + 1, top, ac)


def absorb_all(qs, acc, ka, va):
    for a, b in ((0, ROWS // 2), (ROWS // 2, ROWS + 2 * HALO)):
        acc[a:b, :] = absorb(qs[a:b, :], acc[a:b, :], ka, va)


def empty_rows(rows):
    return jnp.where(lanes((rows, FD)) == HD + 1, FLOOR, 0.0).astype(F32)


def own_body(qa, kv, acc, ka, va):
    load_keys(kv[0:HD, :], kv[HD : 2 * HD, :], ka, va)
    half = ROWS // 2
    for a in (0, half):
        acc[a : a + half, :] = absorb(qa[a : a + half, :], empty_rows(half), ka, va)
    acc[ROWS:, :] = empty_rows(2 * HALO)


def all_queries(qa, left, right, qs):
    qs[0:ROWS, :] = qa[...]
    for n, ref in enumerate((left, right)):
        for i in range(2):
            at = ROWS + n * HALO + i * EXTRA
            qs[at : at + EXTRA, 0:FD] = ref[2 * HD :, i * FD : (i + 1) * FD]
            qs[at : at + EXTRA, FD : 2 * FD] = ref[2 * HD :, (2 + i) * FD : (3 + i) * FD]


def pair_body(step, flags, qa, left, right, kvl, kvr, acc_in, *refs):
    own, (acc, ka, va, qs) = refs[:-4], refs[-4:]
    all_queries(qa, left, right, qs)
    acc[...] = acc_in[...]
    if own:
        load_keys(own[0][0:HD, :], own[0][HD : 2 * HD, :], ka, va)
        acc[ROWS:, :] = absorb(qs[ROWS:, :], acc[ROWS:, :], ka, va)
    for kv, flag in ((kvl, flags[step]), (kvr, flags[8 + step])):

        @pl.when(flag != 0)
        def _():
            load_keys(kv[0:HD, :], kv[HD : 2 * HD, :], ka, va)
            absorb_all(qs, acc, ka, va)


CH = 88
CO = 64


def mid_body(
    flags, qa, left, right, kf, vf, cot, taps, acc_in,
    out_t, kg, qb, qbt, gb, gbt,
    ka, va, qs, acc, cp, cg, ct, tp,
):
    all_queries(qa, left, right, qs)
    acc[...] = acc_in[...]

    @pl.when(flags[4] != 0)
    def _():
        load_keys(kf[...], vf[...], ka, va)
        absorb_all(qs, acc, ka, va)

    a = acc[...]
    weight = a[:, HD : HD + 1]
    ctx = (a / weight).astype(BF).astype(F32)
    ctx = jnp.where(lanes(ctx.shape) < HD, ctx, 0.0)
    lse = a[0:ROWS, HD + 1 : HD + 2] + jnp.log2(weight[0:ROWS])
    keep_l = flags[0] != 0
    keep_r = flags[8] != 0
    cp[0:HALO, :] = jnp.where(keep_l, ctx[ROWS : ROWS + HALO], 0.0)
    cp[HALO : HALO + ROWS, :] = ctx[0:ROWS]
    cp[HALO + ROWS :, :] = jnp.where(keep_r, ctx[ROWS + HALO :], 0.0)
    half = HALO // 2
    cl = left[2 * HD :, 5 * FD : 6 * FD].astype(F32)
    cr = right[2 * HD :, 4 * FD : 5 * FD].astype(F32)
    ct[0:half, :] = jnp.where(keep_l, cl, 0.0)
    ct[half : half + ROWS, :] = cot[...].astype(F32)
    ct[half + ROWS :, :] = jnp.where(keep_r, cr, 0.0)
    tp[...] = taps[...]

    ql = lanes((ROWS, FD))
    l1, l2, l3 = split3(-lse)
    hi = jnp.where(ql == HD, l1, jnp.where(ql == HD + 1, l2, jnp.where(ql == HD + 2, l3, qa[:, 0:FD])))
    qb[:, 0:FD] = hi
    qb[:, FD : 2 * FD] = qa[:, FD : 2 * FD]
    qbt[...] = qb[...].T

    def conv_step(i, _):
        base = pl.multiple_of(i * CH, 8)
        conv = jnp.zeros((CH, FD), F32)
        for j in range(TAPS):
            conv = conv + tp[j : j + 1, :] * cp[pl.ds(base + 1 + j, CH), :]
        sig = jax.nn.sigmoid(conv)
        cg[pl.ds(base, CH), :] = ct[pl.ds(base, CH), :] * sig * (1.0 + conv * (1.0 - sig))
        acc[pl.ds(base, CH), :] = conv * sig
        return 0

    lax.fori_loop(0, (ROWS + HALO) // CH, conv_step, 0)
    res = (cp[HALO : HALO + ROWS, :] + acc[half : half + ROWS, :]).astype(BF)
    out_t[...] = res.T[0:HD, :]

    def grad_step(i, totals):
        base = pl.multiple_of(i * CO, 8)
        g = cg[pl.ds(base + half, CO), :]
        new = []
        grad = ct[pl.ds(base + half, CO), :]
        for j in range(TAPS):
            t = g * cp[pl.ds(base + 17 + j, CO), :]
            new.append(totals[j] + jnp.sum(t.reshape(CO // 8, 8, FD), axis=0))
            grad = grad + tp[j : j + 1, :] * cg[pl.ds(base + 31 - j, CO), :]
        low = grad.astype(BF)
        lowf = low.astype(F32)
        delta = jnp.sum(lowf * cp[pl.ds(base + HALO, CO), :], axis=1, keepdims=True)
        d1, d2, d3 = split3(-delta)
        gl = lanes((CO, FD))
        gb[pl.ds(base, CO), :] = jnp.where(
            gl == HD, d1, jnp.where(gl == HD + 1, d2, jnp.where(gl == HD + 2, d3, low))
        )
        return tuple(new)

    zero = jnp.zeros((8, FD), F32)
    totals = lax.fori_loop(0, ROWS // CO, grad_step, (zero,) * TAPS)
    gbt[...] = gb[...].T
    for j in range(TAPS):
        kg[j : j + 1, :] = jnp.sum(totals[j], axis=0, keepdims=True)
    kg[TAPS:, :] = jnp.zeros((1, FD), F32)


def back_block(k, v, qb, qbt, gb, gbt, dq, kn, vn):
    ones = jnp.ones((FD - HD, ROWS), BF)
    kk = jnp.concatenate([k, ones], axis=0).T
    kn[:, 0:FD] = kk
    kn[:, FD : 2 * FD] = kk
    vn[...] = jnp.concatenate([v, ones], axis=0).T
    p = jnp.exp2(dot(kn[...], qbt[...]))
    ds = (p * dot(vn[...], gbt[...])).astype(BF)
    dv = dot(p.astype(BF), gb[...])
    dk = dot(ds, qb[...])
    dq[...] += dot(k, ds)
    dk = (dk[:, 0:FD] + dk[:, FD : 2 * FD]) * (1.0 / LOG2E)
    return dk.T[0:HD, :], dv.T[0:HD, :]


def far_body(flags, qb, qbt, gb, gbt, kf, vf, dq, dk, dv, kn, vn):
    dq[...] = jnp.zeros_like(dq)

    @pl.when(flags[4] == 0)
    def _():
        dk[...] = jnp.zeros_like(dk)
        dv[...] = jnp.zeros_like(dv)

    @pl.when(flags[4] != 0)
    def _():
        a, b = back_block(kf[...], vf[...], qb, qbt, gb, gbt, dq, kn, vn)
        dk[...] = a.astype(BF)
        dv[...] = b.astype(BF)


def back_pair_body(step, flags, qb, qbt, gb, gbt, kvl, kvr, dq_in, dq, dl, dr, kn, vn):
    dq[...] = dq_in[...]
    for kv, out, flag in ((kvl, dl, flags[step]), (kvr, dr, flags[8 + step])):

        @pl.when(flag == 0)
        def _():
            out[...] = jnp.zeros_like(out)

        @pl.when(flag != 0)
        def _():
            a, b = back_block(kv[0:HD, :], kv[HD : 2 * HD, :], qb, qbt, gb, gbt, dq, kn, vn)
            out[0:HD, :] = a.astype(BF)
            out[HD : 2 * HD, :] = b.astype(BF)


def back_own_body(qb, qbt, gb, gbt, kv, dq_in, dqt, dkv, dq, kn, vn):
    dq[...] = dq_in[...]
    a, b = back_block(kv[0:HD, :], kv[HD : 2 * HD, :], qb, qbt, gb, gbt, dq, kn, vn)
    dqt[...] = (dq[...] * SCALE).astype(BF)
    dkv[0:HD, :] = a
    dkv[HD : 2 * HD, :] = b


KG_ROWS = 32


def split2(x):
    a = x.astype(BF)
    return a, (x - a.astype(F32)).astype(BF)


def put_taps(ref, at, x):
    for n, part in enumerate(split2(x)):
        for i in range(2):
            lane = (2 * n + i) * FD
            ref[at : at + EXTRA, lane : lane + FD] = part[i * EXTRA : (i + 1) * EXTRA]
    ref[at : at + EXTRA, 4 * FD :] = jnp.zeros((EXTRA, 4 * FD), BF)


def get_taps(ref, at):
    p = [ref[at : at + EXTRA, i * FD : (i + 1) * FD].astype(F32) for i in range(4)]
    return jnp.concatenate([p[0] + p[2], p[1] + p[3]], axis=0)


def first_body(yi, dk, dv, k0, k1, k2, k3, to_right, to_left, slots):
    y = yi[0]
    for i, ref in enumerate((k0, k1, k2, k3)):
        slots[(y + 4 - i) % 4] = ref[...]
    total = ((slots[0] + slots[1]) + slots[2]) + slots[3]
    to_right[0:HD, :] = dk[...]
    to_left[0:HD, :] = dv[...]
    put_taps(to_right, HD, total)
    to_left[HD:, :] = to_right[HD:, :]


def merge_body(dl, dr, rl, rr, to_right, to_left):
    if rl.shape[0] == HD + EXTRA:
        to_right[0:HD, :] = (dr[0:HD, :].astype(F32) + rl[0:HD, :].astype(F32)).astype(BF)
        to_right[HD : 2 * HD, :] = dr[HD:, :]
        to_left[0:HD, :] = dl[0:HD, :]
        to_left[HD : 2 * HD, :] = (dl[HD:, :].astype(F32) + rr[0:HD, :].astype(F32)).astype(BF)
    else:
        for out, own, got in ((to_right, dr, rl), (to_left, dl, rr)):
            out[0 : 2 * HD, :] = (own[...].astype(F32) + got[0 : 2 * HD, :].astype(F32)).astype(BF)
    to_right[2 * HD :, :] = rl[rl.shape[0] - EXTRA :, :]
    to_left[2 * HD :, :] = rr[rr.shape[0] - EXTRA :, :]


def send_body(zi, out_t, dqt, dkv, mine, l1, l2, l3, l4, r1, r2, r3, r4, out, slots):
    z = zi[0]
    slots[z] = get_taps(mine, HD)
    for i, ref in enumerate((l1, l2, l3, l4)):
        slots[(z + NB - 1 - i) % NB] = get_taps(ref, HD if i == 0 else 2 * HD)
    for i, ref in enumerate((r1, r2, r3)):
        slots[(z + 1 + i) % NB] = get_taps(ref, HD if i == 0 else 2 * HD)
    total = slots[0]
    for i in range(1, NB):
        total = total + slots[i]
    low = total.astype(BF)
    d = (dkv[...] + l4[0 : 2 * HD, :].astype(F32) + r4[0 : 2 * HD, :].astype(F32)).astype(BF)
    for s in range(NB):
        rows = slice(s * FD, (s + 1) * FD)
        out[s, 0:HD, :] = out_t[:, rows]
        out[s, HD : 2 * HD, :] = dqt[:, rows]
        out[s, 2 * HD : 4 * HD, :] = d[:, rows]
        out[s, 4 * HD :, :] = low


def done_body(r, out, dq, dk, dv, kg):
    for n, ref in enumerate((out, dq, dk, dv)):
        t = jnp.concatenate([r[h, n * HD : (n + 1) * HD, :] for h in range(NB)], axis=0)
        ref[...] = t.T
    for h in range(NB):
        whole = r[h, 4 * HD :, :].astype(F32)
        kg[:, h * HD : (h + 1) * HD] = whole[0:TAPS, 0:HD]


def shift(a, axis, by):
    n = lax.axis_size(axis)
    return lax.ppermute(a, axis, [(i, (i + by) % n) for i in range(n)])


def local(query, key_in, value, lengths, kernel, cotangent):
    z = lax.axis_index("z").astype(jnp.int32).reshape(1)
    head = lax.axis_index(("x", "c")).astype(jnp.int32).reshape(1)
    packed = call(pack_body, "pack", [sds((NB, 4 * HD, FD), BF)], [VM])(
        jnp.stack([query, cotangent, key_in, value])
    )[0]
    got = lax.all_to_all(packed, ("x", "c"), 0, 0, tiled=True)
    block_t = sds((2 * HD, ROWS), BF)
    wide_t = sds((2 * HD + EXTRA, ROWS), BF)
    kv, to_left = call(keys_body, "keys", [wide_t, wide_t], [VM])(got)
    kvl, kvr = [shift(kv, "z", 1)], [shift(to_left, "z", -1)]
    qa, cot, taps, flags = call(
        prep_body, "prep",
        [sds((ROWS, 2 * FD), BF), sds((ROWS, FD), BF), sds((32, FD), F32), sds((16,), jnp.int32)],
        [SM] * 3 + [VM] * 2, out_specs=[VM] * 3 + [SM],
    )(lengths, z, head, got, kernel)
    keys = (pltpu.VMEM((2 * FD, ROWS), BF), pltpu.VMEM((ROWS, FD), BF))
    queries = pltpu.VMEM((ROWS + 2 * HALO, 2 * FD), BF)
    unit = 2 * ROWS * ROWS * 256
    acc_t = sds((ROWS + 2 * HALO, FD), F32)
    acc = call(own_body, "attend_own", [acc_t], [VM] * 2, keys, flops=2 * unit, mib=20)(qa, kv)[0]
    for step in (1, 2, 3):
        acc, kvl[-1], kvr[-1] = lax.optimization_barrier((acc, kvl[-1], kvr[-1]))
        if step < 3:
            kvl.append(shift(kvl[-1], "z", 1))
            kvr.append(shift(kvr[-1], "z", -1))
        else:
            kf = shift(kvl[-1][0:HD], "z", 1)
            vf = shift(kvr[-1][HD : 2 * HD], "z", -1)
        own = (kv,) if step == 1 else ()
        acc = call(
            functools.partial(pair_body, step), f"attend_{step}", [acc_t],
            [SM] + [VM] * (6 + len(own)), keys + (queries,), flops=4 * unit, mib=20,
        )(flags, qa, kvl[0], kvr[0], kvl[step - 1], kvr[step - 1], acc, *own)[0]

    wide = ROWS + 2 * HALO
    out_t, kg, qb, qbt, gb, gbt = call(
        mid_body, "middle",
        [sds((HD, ROWS), BF), sds((32, FD), F32), sds((ROWS, 2 * FD), BF), sds((2 * FD, ROWS), BF),
         sds((ROWS, FD), BF), sds((FD, ROWS), BF)],
        [SM] + [VM] * 8,
        keys + (queries, pltpu.VMEM((wide, FD), F32), pltpu.VMEM((wide, FD), F32),
                pltpu.VMEM((wide, FD), F32), pltpu.VMEM((ROWS + HALO, FD), F32), pltpu.VMEM((32, FD), F32)),
        flops=3 * unit, mib=24,
    )(flags, qa, kvl[0], kvr[0], kf, vf, cot, taps, acc)

    kgs = [kg] + [shift(kg, "grp", i) for i in (1, 2, 3)]
    back = (pltpu.VMEM((ROWS, 2 * FD), BF), pltpu.VMEM((ROWS, FD), BF))
    ops = (qb, qbt, gb, gbt)
    dq_t = sds((HD, ROWS), F32)
    half_t = sds((HD, ROWS), BF)
    dq, dk, dv = call(
        far_body, "back_far", [dq_t, half_t, half_t], [SM] + [VM] * 6, back, flops=5 * unit, mib=32
    )(flags, *ops, kf, vf)
    y = lax.axis_index("grp").astype(jnp.int32).reshape(1)
    far_t = sds((HD + EXTRA, ROWS), BF)
    mine, to_left = call(
        first_body, "first", [far_t, far_t], [SM] + [VM] * 6, (pltpu.VMEM((4, 32, FD), F32),)
    )(y, dk, dv, *kgs)
    rl, rr = [shift(mine, "z", 1)], [shift(to_left, "z", -1)]
    for step in (3, 2, 1):
        dq, dl, dr = call(
            functools.partial(back_pair_body, step), f"back_{step}", [dq_t, block_t, block_t],
            [SM] + [VM] * 7, back, flops=10 * unit, mib=32,
        )(flags, *ops, kvl[step - 1], kvr[step - 1], dq)
        to_right, to_left = call(merge_body, f"merge_{step}", [wide_t, wide_t], [VM] * 4)(
            dl, dr, rl[-1], rr[-1]
        )
        rl.append(shift(to_right, "z", 1))
        rr.append(shift(to_left, "z", -1))
    dqt, dkv = call(
        back_own_body, "back_own", [half_t, sds((2 * HD, ROWS), F32)], [VM] * 6,
        (pltpu.VMEM((HD, ROWS), F32),) + back, flops=5 * unit, mib=32,
    )(*ops, kv, dq)
    packed = call(
        send_body, "pack_out", [sds((NB, 4 * HD + KG_ROWS, FD), BF)], [SM] + [VM] * 12,
        (pltpu.VMEM((NB, 32, FD), F32),),
    )(z, out_t, dqt, dkv, mine, *rl, *rr)[0]
    got = lax.all_to_all(packed, ("x", "c"), 0, 0, tiled=True)
    frames = sds((FD, NB * HD), BF)
    outs = [frames] * 4 + [sds((TAPS, NB * HD), F32)]
    return tuple(call(done_body, "unpack_out", outs, [VM])(got))


def solution(mesh):
    fine = Mesh(mesh.devices.reshape(4, 8, 4, 2), ("grp", "z", "x", "c"))
    frames = P(("grp", "z", "x", "c"), None)
    return jax.shard_map(
        local,
        mesh=fine,
        in_specs=(frames, frames, frames, P("grp", None), P(), frames),
        out_specs=(frames, frames, frames, frames, P()),
        check_vma=False,
    )
```

```python
import functools
import math

import jax
import jax.numpy as jnp
from jax import lax
from jax.experimental import pallas as pl
from jax.experimental.pallas import tpu as pltpu
from jax.sharding import Mesh
from jax.sharding import PartitionSpec as P

F32 = jnp.float32
BF = jnp.bfloat16
HD = 96
FD = 128
NB = 8
ROWS = 1024
HALO = 32
EXTRA = 16
TAPS = 31
SCALE = HD**-0.5
LOG2E = math.log2(math.e)
FLOOR = -1e30

VM = pl.BlockSpec(memory_space=pltpu.VMEM)
SM = pl.BlockSpec(memory_space=pltpu.SMEM)


def params(mib):
    return pltpu.CompilerParams(vmem_limit_bytes=mib * 2**20)


def call(body, name, outs, in_specs, scratch=(), out_specs=None, flops=0, mib=16):
    return pl.pallas_call(
        body,
        name=name,
        out_shape=outs,
        in_specs=in_specs,
        out_specs=out_specs if out_specs is not None else [VM] * len(outs),
        scratch_shapes=list(scratch),
        compiler_params=params(mib),
        cost_estimate=pl.CostEstimate(flops=flops, bytes_accessed=4 * 2**20, transcendentals=0),
    )


def sds(shape, dtype):
    return jax.ShapeDtypeStruct(shape, dtype)


def dot(a, b):
    return jnp.dot(a, b, preferred_element_type=F32)


def lanes(shape):
    return lax.broadcasted_iota(jnp.int32, shape, len(shape) - 1)


def split3(x):
    a = x.astype(BF)
    r = x - a.astype(F32)
    b = r.astype(BF)
    return a, b, (r - b.astype(F32)).astype(BF)


def pack_body(x, out):
    for n in range(4):
        t = x[n].T
        for h in range(NB):
            out[h, n * HD : (n + 1) * HD, :] = t[h * HD : (h + 1) * HD, :]


def scaled(q):
    pad = jnp.zeros((FD - HD, FD), BF)
    q = jnp.concatenate([q, pad], axis=0).T.astype(F32) * (SCALE * LOG2E)
    hi = q.astype(BF)
    return hi, (q - hi.astype(F32)).astype(BF)


def natural(x):
    return jnp.concatenate([x, jnp.zeros((FD - HD, FD), BF)], axis=0).T


def keys_body(r, to_right, to_left):
    for s in range(NB):
        rows = slice(s * FD, (s + 1) * FD)
        to_right[0 : 2 * HD, rows] = r[s, 2 * HD : 4 * HD, :]
        to_left[0 : 2 * HD, rows] = r[s, 2 * HD : 4 * HD, :]
    for ref, s, at in ((to_left, 0, 0), (to_right, NB - 1, FD - HALO)):
        parts = scaled(r[s, 0:HD, :]) + (natural(r[s, HD : 2 * HD, :]),)
        for n, part in enumerate(parts):
            for i in range(2):
                lane = (2 * n + i) * FD
                ref[2 * HD :, lane : lane + FD] = part[at + i * EXTRA : at + (i + 1) * EXTRA]
        ref[2 * HD :, 6 * FD :] = jnp.zeros((EXTRA, 2 * FD), BF)


def prep_body(lengths, zi, head, r, kernel, qa, cot, taps, flags):
    z = zi[0]
    taps[...] = jnp.zeros_like(taps)
    for h in range(NB):

        @pl.when(head[0] == h)
        def _():
            taps[0:TAPS, 0:HD] = kernel[...].astype(F32)[:, h * HD : (h + 1) * HD]

    ends = []
    total = jnp.int32(0)
    for i in range(NB):
        total = total + lengths[0, i]
        ends.append(total)

    def seg(b):
        s = jnp.int32(0)
        for e in ends:
            s = s + (b * ROWS >= e).astype(jnp.int32)
        return s

    own = seg(z)
    for d in range(1, 5):
        flags[d] = (seg((z + NB - d) % NB) == own).astype(jnp.int32)
        flags[8 + d] = (seg((z + d) % NB) == own).astype(jnp.int32)
    flags[0] = jnp.where(z > 0, flags[1], 0)
    flags[8] = jnp.where(z < NB - 1, flags[9], 0)
    for i in (5, 6, 7, 13, 14, 15):
        flags[i] = jnp.int32(0)
    for s in range(NB):
        rows = slice(s * FD, (s + 1) * FD)
        hi, lo = scaled(r[s, 0:HD, :])
        qa[rows, 0:FD] = hi
        qa[rows, FD : 2 * FD] = lo
        cot[rows, :] = natural(r[s, HD : 2 * HD, :])


def load_keys(k, v, ka, va):
    zero = jnp.zeros((FD - HD, ROWS), BF)
    ka[0:HD, :] = k
    ka[HD:FD, :] = zero
    ka[FD : FD + HD, :] = k
    ka[FD + HD :, :] = zero
    one = (lax.broadcasted_iota(jnp.int32, (FD - HD, ROWS), 0) == 0).astype(F32).astype(BF)
    va[...] = jnp.concatenate([v, one], axis=0).T


def absorb(q, ac, ka, va):
    peak = ac[:, HD + 1 : HD + 2]
    s = dot(q, ka[...])
    top = jnp.maximum(peak, jnp.max(s, axis=1, keepdims=True))
    p = jnp.exp2(s - top).astype(BF)
    ac = ac * jnp.exp2(peak - top) + dot(p, va[...])
    return jnp.where(lanes(ac.shape) == HD + 1, top, ac)


def absorb_all(qs, acc, ka, va):
    for a, b in ((0, ROWS // 2), (ROWS // 2, ROWS + 2 * HALO)):
        acc[a:b, :] = absorb(qs[a:b, :], acc[a:b, :], ka, va)


def empty_rows(rows):
    return jnp.where(lanes((rows, FD)) == HD + 1, FLOOR, 0.0).astype(F32)


def own_body(qa, kv, acc, ka, va):
    load_keys(kv[0:HD, :], kv[HD : 2 * HD, :], ka, va)
    half = ROWS // 2
    for a in (0, half):
        acc[a : a + half, :] = absorb(qa[a : a + half, :], empty_rows(half), ka, va)
    acc[ROWS:, :] = empty_rows(2 * HALO)


def all_queries(qa, left, right, qs):
    qs[0:ROWS, :] = qa[...]
    for n, ref in enumerate((left, right)):
        for i in range(2):
            at = ROWS + n * HALO + i * EXTRA
            qs[at : at + EXTRA, 0:FD] = ref[2 * HD :, i * FD : (i + 1) * FD]
            qs[at : at + EXTRA, FD : 2 * FD] = ref[2 * HD :, (2 + i) * FD : (3 + i) * FD]


def pair_body(step, flags, qa, left, right, kvl, kvr, acc_in, *refs):
    own, (acc, ka, va, qs) = refs[:-4], refs[-4:]
    all_queries(qa, left, right, qs)
    acc[...] = acc_in[...]
    if own:
        load_keys(own[0][0:HD, :], own[0][HD : 2 * HD, :], ka, va)
        acc[ROWS:, :] = absorb(qs[ROWS:, :], acc[ROWS:, :], ka, va)
    for kv, flag in ((kvl, flags[step]), (kvr, flags[8 + step])):

        @pl.when(flag != 0)
        def _():
            load_keys(kv[0:HD, :], kv[HD : 2 * HD, :], ka, va)
            absorb_all(qs, acc, ka, va)


CH = 88
CO = 64


def mid_body(
    flags, qa, left, right, kf, vf, cot, taps, acc_in,
    out_t, kg, qb, qbt, gb, gbt,
    ka, va, qs, acc, cp, cg, ct, tp,
):
    all_queries(qa, left, right, qs)
    acc[...] = acc_in[...]

    @pl.when(flags[4] != 0)
    def _():
        load_keys(kf[...], vf[...], ka, va)
        absorb_all(qs, acc, ka, va)

    a = acc[...]
    weight = a[:, HD : HD + 1]
    ctx = (a / weight).astype(BF).astype(F32)
    ctx = jnp.where(lanes(ctx.shape) < HD, ctx, 0.0)
    lse = a[0:ROWS, HD + 1 : HD + 2] + jnp.log2(weight[0:ROWS])
    keep_l = flags[0] != 0
    keep_r = flags[8] != 0
    cp[0:HALO, :] = jnp.where(keep_l, ctx[ROWS : ROWS + HALO], 0.0)
    cp[HALO : HALO + ROWS, :] = ctx[0:ROWS]
    cp[HALO + ROWS :, :] = jnp.where(keep_r, ctx[ROWS + HALO :], 0.0)
    half = HALO // 2
    cl = left[2 * HD :, 5 * FD : 6 * FD].astype(F32)
    cr = right[2 * HD :, 4 * FD : 5 * FD].astype(F32)
    ct[0:half, :] = jnp.where(keep_l, cl, 0.0)
    ct[half : half + ROWS, :] = cot[...].astype(F32)
    ct[half + ROWS :, :] = jnp.where(keep_r, cr, 0.0)
    tp[...] = taps[...]

    ql = lanes((ROWS, FD))
    l1, l2, l3 = split3(-lse)
    hi = jnp.where(ql == HD, l1, jnp.where(ql == HD + 1, l2, jnp.where(ql == HD + 2, l3, qa[:, 0:FD])))
    qb[:, 0:FD] = hi
    qb[:, FD : 2 * FD] = qa[:, FD : 2 * FD]
    qbt[...] = qb[...].T

    def conv_step(i, _):
        base = pl.multiple_of(i * CH, 8)
        conv = jnp.zeros((CH, FD), F32)
        for j in range(TAPS):
            conv = conv + tp[j : j + 1, :] * cp[pl.ds(base + 1 + j, CH), :]
        sig = jax.nn.sigmoid(conv)
        cg[pl.ds(base, CH), :] = ct[pl.ds(base, CH), :] * sig * (1.0 + conv * (1.0 - sig))
        acc[pl.ds(base, CH), :] = conv * sig
        return 0

    lax.fori_loop(0, (ROWS + HALO) // CH, conv_step, 0)
    res = (cp[HALO : HALO + ROWS, :] + acc[half : half + ROWS, :]).astype(BF)
    out_t[...] = res.T[0:HD, :]

    def grad_step(i, totals):
        base = pl.multiple_of(i * CO, 8)
        g = cg[pl.ds(base + half, CO), :]
        new = []
        grad = ct[pl.ds(base + half, CO), :]
        for j in range(TAPS):
            t = g * cp[pl.ds(base + 17 + j, CO), :]
            new.append(totals[j] + jnp.sum(t.reshape(CO // 8, 8, FD), axis=0))
            grad = grad + tp[j : j + 1, :] * cg[pl.ds(base + 31 - j, CO), :]
        low = grad.astype(BF)
        lowf = low.astype(F32)
        delta = jnp.sum(lowf * cp[pl.ds(base + HALO, CO), :], axis=1, keepdims=True)
        d1, d2, d3 = split3(-delta)
        gl = lanes((CO, FD))
        gb[pl.ds(base, CO), :] = jnp.where(
            gl == HD, d1, jnp.where(gl == HD + 1, d2, jnp.where(gl == HD + 2, d3, low))
        )
        return tuple(new)

    zero = jnp.zeros((8, FD), F32)
    totals = lax.fori_loop(0, ROWS // CO, grad_step, (zero,) * TAPS)
    gbt[...] = gb[...].T
    for j in range(TAPS):
        kg[j : j + 1, :] = jnp.sum(totals[j], axis=0, keepdims=True)
    kg[TAPS:, :] = jnp.zeros((1, FD), F32)


def back_block(k, v, qb, qbt, gb, gbt, dq, kn, vn):
    ones = jnp.ones((FD - HD, ROWS), BF)
    kk = jnp.concatenate([k, ones], axis=0).T
    kn[:, 0:FD] = kk
    kn[:, FD : 2 * FD] = kk
    vn[...] = jnp.concatenate([v, ones], axis=0).T
    p = jnp.exp2(dot(kn[...], qbt[...]))
    ds = (p * dot(vn[...], gbt[...])).astype(BF)
    dv = dot(p.astype(BF), gb[...])
    dk = dot(ds, qb[...])
    dq[...] += dot(k, ds)
    dk = (dk[:, 0:FD] + dk[:, FD : 2 * FD]) * (1.0 / LOG2E)
    return dk.T[0:HD, :], dv.T[0:HD, :]


def far_body(flags, qb, qbt, gb, gbt, kf, vf, dq, dk, dv, kn, vn):
    dq[...] = jnp.zeros_like(dq)

    @pl.when(flags[4] == 0)
    def _():
        dk[...] = jnp.zeros_like(dk)
        dv[...] = jnp.zeros_like(dv)

    @pl.when(flags[4] != 0)
    def _():
        a, b = back_block(kf[...], vf[...], qb, qbt, gb, gbt, dq, kn, vn)
        dk[...] = a.astype(BF)
        dv[...] = b.astype(BF)


def back_pair_body(step, flags, qb, qbt, gb, gbt, kvl, kvr, dq_in, dq, dl, dr, kn, vn):
    dq[...] = dq_in[...]
    for kv, out, flag in ((kvl, dl, flags[step]), (kvr, dr, flags[8 + step])):

        @pl.when(flag == 0)
        def _():
            out[...] = jnp.zeros_like(out)

        @pl.when(flag != 0)
        def _():
            a, b = back_block(kv[0:HD, :], kv[HD : 2 * HD, :], qb, qbt, gb, gbt, dq, kn, vn)
            out[0:HD, :] = a.astype(BF)
            out[HD : 2 * HD, :] = b.astype(BF)


def back_own_body(qb, qbt, gb, gbt, kv, dq_in, dqt, dkv, dq, kn, vn):
    dq[...] = dq_in[...]
    a, b = back_block(kv[0:HD, :], kv[HD : 2 * HD, :], qb, qbt, gb, gbt, dq, kn, vn)
    dqt[...] = (dq[...] * SCALE).astype(BF)
    dkv[0:HD, :] = a
    dkv[HD : 2 * HD, :] = b


KG_ROWS = 32


def split2(x):
    a = x.astype(BF)
    return a, (x - a.astype(F32)).astype(BF)


def put_taps(ref, at, x):
    for n, part in enumerate(split2(x)):
        for i in range(2):
            lane = (2 * n + i) * FD
            ref[at : at + EXTRA, lane : lane + FD] = part[i * EXTRA : (i + 1) * EXTRA]
    ref[at : at + EXTRA, 4 * FD :] = jnp.zeros((EXTRA, 4 * FD), BF)


def get_taps(ref, at):
    p = [ref[at : at + EXTRA, i * FD : (i + 1) * FD].astype(F32) for i in range(4)]
    return jnp.concatenate([p[0] + p[2], p[1] + p[3]], axis=0)


def first_body(dk, dv, kg, to_right, to_left):
    to_right[0:HD, :] = dk[...]
    to_left[0:HD, :] = dv[...]
    put_taps(to_right, HD, kg[...])
    to_left[HD:, :] = to_right[HD:, :]


def line_body(zi, mine, l1, l2, l3, l4, r1, r2, r3, out, slots):
    z = zi[0]
    slots[z] = get_taps(mine, HD)
    for i, (ref, at) in enumerate(((l1, HD), (l2, 2 * HD), (l3, 2 * HD), (l4, 0))):
        slots[(z + NB - 1 - i) % NB] = get_taps(ref, at)
    for i, (ref, at) in enumerate(((r1, HD), (r2, 2 * HD), (r3, 2 * HD))):
        slots[(z + 1 + i) % NB] = get_taps(ref, at)
    total = slots[0]
    for i in range(1, NB):
        total = total + slots[i]
    out[...] = total


def merge_body(dl, dr, rl, rr, to_right, to_left):
    if rl.shape[0] == HD + EXTRA:
        to_right[0:HD, :] = (dr[0:HD, :].astype(F32) + rl[0:HD, :].astype(F32)).astype(BF)
        to_right[HD : 2 * HD, :] = dr[HD:, :]
        to_left[0:HD, :] = dl[0:HD, :]
        to_left[HD : 2 * HD, :] = (dl[HD:, :].astype(F32) + rr[0:HD, :].astype(F32)).astype(BF)
    else:
        for out, own, got in ((to_right, dr, rl), (to_left, dl, rr)):
            out[0 : 2 * HD, :] = (own[...].astype(F32) + got[0 : 2 * HD, :].astype(F32)).astype(BF)
    if to_right.shape[0] > 2 * HD:
        to_right[2 * HD :, :] = rl[rl.shape[0] - EXTRA :, :]
        to_left[2 * HD :, :] = rr[rr.shape[0] - EXTRA :, :]


def send_body(yi, out_t, dqt, dkv, l4, r4, k0, k1, k2, k3, out, slots):
    y = yi[0]
    for i, ref in enumerate((k0, k1, k2, k3)):
        slots[(y + 4 - i) % 4] = ref[...]
    low = (((slots[0] + slots[1]) + slots[2]) + slots[3]).astype(BF)
    d = (dkv[...] + l4[0 : 2 * HD, :].astype(F32) + r4[0 : 2 * HD, :].astype(F32)).astype(BF)
    for s in range(NB):
        rows = slice(s * FD, (s + 1) * FD)
        out[s, 0:HD, :] = out_t[:, rows]
        out[s, HD : 2 * HD, :] = dqt[:, rows]
        out[s, 2 * HD : 4 * HD, :] = d[:, rows]
        out[s, 4 * HD :, :] = low


def done_body(r, out, dq, dk, dv, kg):
    for n, ref in enumerate((out, dq, dk, dv)):
        t = jnp.concatenate([r[h, n * HD : (n + 1) * HD, :] for h in range(NB)], axis=0)
        ref[...] = t.T
    for h in range(NB):
        whole = r[h, 4 * HD :, :].astype(F32)
        kg[:, h * HD : (h + 1) * HD] = whole[0:TAPS, 0:HD]


def shift(a, axis, by):
    n = lax.axis_size(axis)
    return lax.ppermute(a, axis, [(i, (i + by) % n) for i in range(n)])


def local(query, key_in, value, lengths, kernel, cotangent):
    z = lax.axis_index("z").astype(jnp.int32).reshape(1)
    head = lax.axis_index(("x", "c")).astype(jnp.int32).reshape(1)
    packed = call(pack_body, "pack", [sds((NB, 4 * HD, FD), BF)], [VM])(
        jnp.stack([query, cotangent, key_in, value])
    )[0]
    got = lax.all_to_all(packed, ("x", "c"), 0, 0, tiled=True)
    block_t = sds((2 * HD, ROWS), BF)
    wide_t = sds((2 * HD + EXTRA, ROWS), BF)
    kv, to_left = call(keys_body, "keys", [wide_t, wide_t], [VM])(got)
    kvl, kvr = [shift(kv, "z", 1)], [shift(to_left, "z", -1)]
    qa, cot, taps, flags = call(
        prep_body, "prep",
        [sds((ROWS, 2 * FD), BF), sds((ROWS, FD), BF), sds((32, FD), F32), sds((16,), jnp.int32)],
        [SM] * 3 + [VM] * 2, out_specs=[VM] * 3 + [SM],
    )(lengths, z, head, got, kernel)
    keys = (pltpu.VMEM((2 * FD, ROWS), BF), pltpu.VMEM((ROWS, FD), BF))
    queries = pltpu.VMEM((ROWS + 2 * HALO, 2 * FD), BF)
    unit = 2 * ROWS * ROWS * 256
    acc_t = sds((ROWS + 2 * HALO, FD), F32)
    acc = call(own_body, "attend_own", [acc_t], [VM] * 2, keys, flops=2 * unit, mib=20)(qa, kv)[0]
    for step in (1, 2, 3):
        acc, kvl[-1], kvr[-1] = lax.optimization_barrier((acc, kvl[-1], kvr[-1]))
        if step < 3:
            kvl.append(shift(kvl[-1], "z", 1))
            kvr.append(shift(kvr[-1], "z", -1))
        else:
            kf = shift(kvl[-1][0:HD], "z", 1)
            vf = shift(kvr[-1][HD : 2 * HD], "z", -1)
        own = (kv,) if step == 1 else ()
        acc = call(
            functools.partial(pair_body, step), f"attend_{step}", [acc_t],
            [SM] + [VM] * (6 + len(own)), keys + (queries,), flops=4 * unit, mib=20,
        )(flags, qa, kvl[0], kvr[0], kvl[step - 1], kvr[step - 1], acc, *own)[0]

    wide = ROWS + 2 * HALO
    out_t, kg, qb, qbt, gb, gbt = call(
        mid_body, "middle",
        [sds((HD, ROWS), BF), sds((32, FD), F32), sds((ROWS, 2 * FD), BF), sds((2 * FD, ROWS), BF),
         sds((ROWS, FD), BF), sds((FD, ROWS), BF)],
        [SM] + [VM] * 8,
        keys + (queries, pltpu.VMEM((wide, FD), F32), pltpu.VMEM((wide, FD), F32),
                pltpu.VMEM((wide, FD), F32), pltpu.VMEM((ROWS + HALO, FD), F32), pltpu.VMEM((32, FD), F32)),
        flops=3 * unit, mib=24,
    )(flags, qa, kvl[0], kvr[0], kf, vf, cot, taps, acc)

    back = (pltpu.VMEM((ROWS, 2 * FD), BF), pltpu.VMEM((ROWS, FD), BF))
    ops = (qb, qbt, gb, gbt)
    dq_t = sds((HD, ROWS), F32)
    half_t = sds((HD, ROWS), BF)
    dq, dk, dv = call(
        far_body, "back_far", [dq_t, half_t, half_t], [SM] + [VM] * 6, back, flops=5 * unit, mib=32
    )(flags, *ops, kf, vf)
    y = lax.axis_index("grp").astype(jnp.int32).reshape(1)
    far_t = sds((HD + EXTRA, ROWS), BF)
    mine, to_left = call(first_body, "first", [far_t, far_t], [VM] * 3)(dk, dv, kg)
    rl, rr = [shift(mine, "z", 1)], [shift(to_left, "z", -1)]
    for step in (3, 2, 1):
        dq, dl, dr = call(
            functools.partial(back_pair_body, step), f"back_{step}", [dq_t, block_t, block_t],
            [SM] + [VM] * 7, back, flops=10 * unit, mib=32,
        )(flags, *ops, kvl[step - 1], kvr[step - 1], dq)
        to_right, to_left = call(merge_body, f"merge_{step}", [wide_t if step > 1 else block_t] * 2, [VM] * 4)(
            dl, dr, rl[-1], rr[-1]
        )
        rl.append(shift(to_right, "z", 1))
        rr.append(shift(to_left, "z", -1))
    dqt, dkv = call(
        back_own_body, "back_own", [half_t, sds((2 * HD, ROWS), F32)], [VM] * 6,
        (pltpu.VMEM((HD, ROWS), F32),) + back, flops=5 * unit, mib=32,
    )(*ops, kv, dq)
    kg = call(line_body, "line", [sds((32, FD), F32)], [SM] + [VM] * 8, (pltpu.VMEM((NB, 32, FD), F32),))(
        z, mine, *rl[:3], shift(rl[2][2 * HD :], "z", 1), *rr[:3]
    )[0]
    kg, dqt = lax.optimization_barrier((kg, dqt))
    kgs = [kg] + [shift(kg, "grp", i) for i in (1, 2, 3)]
    packed = call(
        send_body, "pack_out", [sds((NB, 4 * HD + KG_ROWS, FD), BF)], [SM] + [VM] * 9,
        (pltpu.VMEM((4, 32, FD), F32),),
    )(y, out_t, dqt, dkv, rl[3], rr[3], *kgs)[0]
    got = lax.all_to_all(packed, ("x", "c"), 0, 0, tiled=True)
    frames = sds((FD, NB * HD), BF)
    outs = [frames] * 4 + [sds((TAPS, NB * HD), F32)]
    return tuple(call(done_body, "unpack_out", outs, [VM])(got))


def solution(mesh):
    fine = Mesh(mesh.devices.reshape(4, 8, 4, 2), ("grp", "z", "x", "c"))
    frames = P(("grp", "z", "x", "c"), None)
    return jax.shard_map(
        local,
        mesh=fine,
        in_specs=(frames, frames, frames, P("grp", None), P(), frames),
        out_specs=(frames, frames, frames, frames, P()),
        check_vma=False,
    )
```

```python
import functools
import math

import jax
import jax.numpy as jnp
from jax import lax
from jax.experimental import pallas as pl
from jax.experimental.pallas import tpu as pltpu
from jax.sharding import Mesh
from jax.sharding import PartitionSpec as P

F32 = jnp.float32
BF = jnp.bfloat16
HD = 96
FD = 128
NB = 8
ROWS = 1024
HALO = 32
EXTRA = 16
TAPS = 31
SCALE = HD**-0.5
LOG2E = math.log2(math.e)
FLOOR = -1e30

VM = pl.BlockSpec(memory_space=pltpu.VMEM)
SM = pl.BlockSpec(memory_space=pltpu.SMEM)


def params(mib):
    return pltpu.CompilerParams(vmem_limit_bytes=mib * 2**20)


def call(body, name, outs, in_specs, scratch=(), out_specs=None, flops=0, mib=16):
    return pl.pallas_call(
        body,
        name=name,
        out_shape=outs,
        in_specs=in_specs,
        out_specs=out_specs if out_specs is not None else [VM] * len(outs),
        scratch_shapes=list(scratch),
        compiler_params=params(mib),
        cost_estimate=pl.CostEstimate(flops=flops, bytes_accessed=4 * 2**20, transcendentals=0),
    )


def sds(shape, dtype):
    return jax.ShapeDtypeStruct(shape, dtype)


def dot(a, b):
    return jnp.dot(a, b, preferred_element_type=F32)


def lanes(shape):
    return lax.broadcasted_iota(jnp.int32, shape, len(shape) - 1)


def split3(x):
    a = x.astype(BF)
    r = x - a.astype(F32)
    b = r.astype(BF)
    return a, b, (r - b.astype(F32)).astype(BF)


def pack_body(x, out):
    for n in range(4):
        t = x[n].T
        for h in range(NB):
            out[h, n * HD : (n + 1) * HD, :] = t[h * HD : (h + 1) * HD, :]


def scaled(q):
    pad = jnp.zeros((FD - HD, FD), BF)
    q = jnp.concatenate([q, pad], axis=0).T.astype(F32) * (SCALE * LOG2E)
    hi = q.astype(BF)
    return hi, (q - hi.astype(F32)).astype(BF)


def natural(x):
    return jnp.concatenate([x, jnp.zeros((FD - HD, FD), BF)], axis=0).T


def keys_body(r, to_right, to_left):
    for s in range(NB):
        rows = slice(s * FD, (s + 1) * FD)
        to_right[0 : 2 * HD, rows] = r[s, 2 * HD : 4 * HD, :]
        to_left[0 : 2 * HD, rows] = r[s, 2 * HD : 4 * HD, :]
    for ref, s, at in ((to_left, 0, 0), (to_right, NB - 1, FD - HALO)):
        parts = scaled(r[s, 0:HD, :]) + (natural(r[s, HD : 2 * HD, :]),)
        for n, part in enumerate(parts):
            for i in range(2):
                lane = (2 * n + i) * FD
                ref[2 * HD :, lane : lane + FD] = part[at + i * EXTRA : at + (i + 1) * EXTRA]
        ref[2 * HD :, 6 * FD :] = jnp.zeros((EXTRA, 2 * FD), BF)


def prep_body(lengths, zi, head, r, kernel, qa, cot, taps, flags):
    z = zi[0]
    taps[...] = jnp.zeros_like(taps)
    for h in range(NB):

        @pl.when(head[0] == h)
        def _():
            taps[0:TAPS, 0:HD] = kernel[...].astype(F32)[:, h * HD : (h + 1) * HD]

    ends = []
    total = jnp.int32(0)
    for i in range(NB):
        total = total + lengths[0, i]
        ends.append(total)

    def seg(b):
        s = jnp.int32(0)
        for e in ends:
            s = s + (b * ROWS >= e).astype(jnp.int32)
        return s

    own = seg(z)
    for d in range(1, 5):
        flags[d] = (seg((z + NB - d) % NB) == own).astype(jnp.int32)
        flags[8 + d] = (seg((z + d) % NB) == own).astype(jnp.int32)
    flags[0] = jnp.where(z > 0, flags[1], 0)
    flags[8] = jnp.where(z < NB - 1, flags[9], 0)
    for i in (5, 6, 7, 13, 14, 15):
        flags[i] = jnp.int32(0)
    for s in range(NB):
        rows = slice(s * FD, (s + 1) * FD)
        hi, lo = scaled(r[s, 0:HD, :])
        qa[rows, 0:FD] = hi
        qa[rows, FD : 2 * FD] = lo
        cot[rows, :] = natural(r[s, HD : 2 * HD, :])


def load_keys(k, v, ka, va):
    zero = jnp.zeros((FD - HD, ROWS), BF)
    ka[0:HD, :] = k
    ka[HD:FD, :] = zero
    ka[FD : FD + HD, :] = k
    ka[FD + HD :, :] = zero
    one = (lax.broadcasted_iota(jnp.int32, (FD - HD, ROWS), 0) == 0).astype(F32).astype(BF)
    va[...] = jnp.concatenate([v, one], axis=0).T


def absorb(q, ac, ka, va):
    peak = ac[:, HD + 1 : HD + 2]
    s = dot(q, ka[...])
    top = jnp.maximum(peak, jnp.max(s, axis=1, keepdims=True))
    p = jnp.exp2(s - top).astype(BF)
    ac = ac * jnp.exp2(peak - top) + dot(p, va[...])
    return jnp.where(lanes(ac.shape) == HD + 1, top, ac)


def absorb_all(qs, acc, ka, va):
    for a, b in ((0, ROWS // 2), (ROWS // 2, ROWS + 2 * HALO)):
        acc[a:b, :] = absorb(qs[a:b, :], acc[a:b, :], ka, va)


def empty_rows(rows):
    return jnp.where(lanes((rows, FD)) == HD + 1, FLOOR, 0.0).astype(F32)


def own_body(qa, kv, acc, ka, va):
    load_keys(kv[0:HD, :], kv[HD : 2 * HD, :], ka, va)
    half = ROWS // 2
    for a in (0, half):
        acc[a : a + half, :] = absorb(qa[a : a + half, :], empty_rows(half), ka, va)
    acc[ROWS:, :] = empty_rows(2 * HALO)


def all_queries(qa, left, right, qs):
    qs[0:ROWS, :] = qa[...]
    for n, ref in enumerate((left, right)):
        for i in range(2):
            at = ROWS + n * HALO + i * EXTRA
            qs[at : at + EXTRA, 0:FD] = ref[2 * HD :, i * FD : (i + 1) * FD]
            qs[at : at + EXTRA, FD : 2 * FD] = ref[2 * HD :, (2 + i) * FD : (3 + i) * FD]


def pair_body(step, flags, qa, left, right, kvl, kvr, acc_in, *refs):
    own, (acc, ka, va, qs) = refs[:-4], refs[-4:]
    all_queries(qa, left, right, qs)
    acc[...] = acc_in[...]
    if own:
        load_keys(own[0][0:HD, :], own[0][HD : 2 * HD, :], ka, va)
        acc[ROWS:, :] = absorb(qs[ROWS:, :], acc[ROWS:, :], ka, va)
    for kv, flag in ((kvl, flags[step]), (kvr, flags[8 + step])):

        @pl.when(flag != 0)
        def _():
            load_keys(kv[0:HD, :], kv[HD : 2 * HD, :], ka, va)
            absorb_all(qs, acc, ka, va)


CH = 88
CO = 64


def mid_body(
    flags, qa, left, right, kf, vf, cot, taps, acc_in,
    out_t, kg, qb, qbt, gb, gbt,
    ka, va, qs, acc, cp, cg, ct, tp,
):
    all_queries(qa, left, right, qs)
    acc[...] = acc_in[...]

    @pl.when(flags[4] != 0)
    def _():
        load_keys(kf[...], vf[...], ka, va)
        absorb_all(qs, acc, ka, va)

    a = acc[...]
    weight = a[:, HD : HD + 1]
    ctx = (a * (1.0 / weight)).astype(BF).astype(F32)
    ctx = jnp.where(lanes(ctx.shape) < HD, ctx, 0.0)
    lse = a[0:ROWS, HD + 1 : HD + 2] + jnp.log2(weight[0:ROWS])
    keep_l = flags[0] != 0
    keep_r = flags[8] != 0
    cp[0:HALO, :] = jnp.where(keep_l, ctx[ROWS : ROWS + HALO], 0.0)
    cp[HALO : HALO + ROWS, :] = ctx[0:ROWS]
    cp[HALO + ROWS :, :] = jnp.where(keep_r, ctx[ROWS + HALO :], 0.0)
    half = HALO // 2
    cl = left[2 * HD :, 5 * FD : 6 * FD].astype(F32)
    cr = right[2 * HD :, 4 * FD : 5 * FD].astype(F32)
    ct[0:half, :] = jnp.where(keep_l, cl, 0.0)
    ct[half : half + ROWS, :] = cot[...].astype(F32)
    ct[half + ROWS :, :] = jnp.where(keep_r, cr, 0.0)
    tp[...] = taps[...]

    ql = lanes((ROWS, FD))
    l1, l2, l3 = split3(-lse)
    hi = jnp.where(ql == HD, l1, jnp.where(ql == HD + 1, l2, jnp.where(ql == HD + 2, l3, qa[:, 0:FD])))
    qb[:, 0:FD] = hi
    qb[:, FD : 2 * FD] = qa[:, FD : 2 * FD]
    qbt[...] = qb[...].T

    def conv_step(i, _):
        base = pl.multiple_of(i * CH, 8)
        conv = jnp.zeros((CH, FD), F32)
        for j in range(TAPS):
            conv = conv + tp[j : j + 1, :] * cp[pl.ds(base + 1 + j, CH), :]
        sig = jax.nn.sigmoid(conv)
        cg[pl.ds(base, CH), :] = ct[pl.ds(base, CH), :] * sig * (1.0 + conv * (1.0 - sig))
        acc[pl.ds(base, CH), :] = conv * sig
        return 0

    lax.fori_loop(0, (ROWS + HALO) // CH, conv_step, 0)
    res = (cp[HALO : HALO + ROWS, :] + acc[half : half + ROWS, :]).astype(BF)
    out_t[...] = res.T[0:HD, :]

    def grad_step(i, totals):
        base = pl.multiple_of(i * CO, 8)
        g = cg[pl.ds(base + half, CO), :]
        new = []
        grad = ct[pl.ds(base + half, CO), :]
        for j in range(TAPS):
            t = g * cp[pl.ds(base + 17 + j, CO), :]
            new.append(totals[j] + jnp.sum(t.reshape(CO // 8, 8, FD), axis=0))
            grad = grad + tp[j : j + 1, :] * cg[pl.ds(base + 31 - j, CO), :]
        low = grad.astype(BF)
        lowf = low.astype(F32)
        delta = jnp.sum(lowf * cp[pl.ds(base + HALO, CO), :], axis=1, keepdims=True)
        d1, d2, d3 = split3(-delta)
        gl = lanes((CO, FD))
        gb[pl.ds(base, CO), :] = jnp.where(
            gl == HD, d1, jnp.where(gl == HD + 1, d2, jnp.where(gl == HD + 2, d3, low))
        )
        return tuple(new)

    zero = jnp.zeros((8, FD), F32)
    totals = lax.fori_loop(0, ROWS // CO, grad_step, (zero,) * TAPS)
    gbt[...] = gb[...].T
    for j in range(TAPS):
        kg[j : j + 1, :] = jnp.sum(totals[j], axis=0, keepdims=True)
    kg[TAPS:, :] = jnp.zeros((1, FD), F32)


def back_block(k, v, qb, qbt, gb, gbt, dq, kn, vn):
    ones = jnp.ones((FD - HD, ROWS), BF)
    kk = jnp.concatenate([k, ones], axis=0).T
    kn[:, 0:FD] = kk
    kn[:, FD : 2 * FD] = kk
    vn[...] = jnp.concatenate([v, ones], axis=0).T
    p = jnp.exp2(dot(kn[...], qbt[...]))
    ds = (p * dot(vn[...], gbt[...])).astype(BF)
    dv = dot(p.astype(BF), gb[...])
    dk = dot(ds, qb[...])
    dq[...] += dot(k, ds)
    dk = (dk[:, 0:FD] + dk[:, FD : 2 * FD]) * (1.0 / LOG2E)
    return dk.T[0:HD, :], dv.T[0:HD, :]


def far_body(flags, qb, qbt, gb, gbt, kf, vf, dq, dk, dv, kn, vn):
    dq[...] = jnp.zeros_like(dq)

    @pl.when(flags[4] == 0)
    def _():
        dk[...] = jnp.zeros_like(dk)
        dv[...] = jnp.zeros_like(dv)

    @pl.when(flags[4] != 0)
    def _():
        a, b = back_block(kf[...], vf[...], qb, qbt, gb, gbt, dq, kn, vn)
        dk[...] = a.astype(BF)
        dv[...] = b.astype(BF)


def back_pair_body(step, flags, qb, qbt, gb, gbt, kvl, kvr, dq_in, dq, dl, dr, kn, vn):
    dq[...] = dq_in[...]
    for kv, out, flag in ((kvl, dl, flags[step]), (kvr, dr, flags[8 + step])):

        @pl.when(flag == 0)
        def _():
            out[...] = jnp.zeros_like(out)

        @pl.when(flag != 0)
        def _():
            a, b = back_block(kv[0:HD, :], kv[HD : 2 * HD, :], qb, qbt, gb, gbt, dq, kn, vn)
            out[0:HD, :] = a.astype(BF)
            out[HD : 2 * HD, :] = b.astype(BF)


def back_own_body(qb, qbt, gb, gbt, kv, dq_in, dqt, dkv, dq, kn, vn):
    dq[...] = dq_in[...]
    a, b = back_block(kv[0:HD, :], kv[HD : 2 * HD, :], qb, qbt, gb, gbt, dq, kn, vn)
    dqt[...] = (dq[...] * SCALE).astype(BF)
    dkv[0:HD, :] = a
    dkv[HD : 2 * HD, :] = b


KG_ROWS = 32


def split2(x):
    a = x.astype(BF)
    return a, (x - a.astype(F32)).astype(BF)


def put_taps(ref, at, x):
    for n, part in enumerate(split2(x)):
        for i in range(2):
            lane = (2 * n + i) * FD
            ref[at : at + EXTRA, lane : lane + FD] = part[i * EXTRA : (i + 1) * EXTRA]
    ref[at : at + EXTRA, 4 * FD :] = jnp.zeros((EXTRA, 4 * FD), BF)


def get_taps(ref, at):
    p = [ref[at : at + EXTRA, i * FD : (i + 1) * FD].astype(F32) for i in range(4)]
    return jnp.concatenate([p[0] + p[2], p[1] + p[3]], axis=0)


def first_body(dk, dv, kg, to_right, to_left):
    to_right[0:HD, :] = dk[...]
    to_left[0:HD, :] = dv[...]
    put_taps(to_right, HD, kg[...])
    to_left[HD:, :] = to_right[HD:, :]


def line_body(zi, mine, l1, l2, l3, l4, r1, r2, r3, out, slots):
    z = zi[0]
    slots[z] = get_taps(mine, HD)
    for i, (ref, at) in enumerate(((l1, HD), (l2, 2 * HD), (l3, 2 * HD), (l4, 0))):
        slots[(z + NB - 1 - i) % NB] = get_taps(ref, at)
    for i, (ref, at) in enumerate(((r1, HD), (r2, 2 * HD), (r3, 2 * HD))):
        slots[(z + 1 + i) % NB] = get_taps(ref, at)
    total = slots[0]
    for i in range(1, NB):
        total = total + slots[i]
    out[...] = total


def merge_body(dl, dr, rl, rr, to_right, to_left):
    if rl.shape[0] == HD + EXTRA:
        to_right[0:HD, :] = (dr[0:HD, :].astype(F32) + rl[0:HD, :].astype(F32)).astype(BF)
        to_right[HD : 2 * HD, :] = dr[HD:, :]
        to_left[0:HD, :] = dl[0:HD, :]
        to_left[HD : 2 * HD, :] = (dl[HD:, :].astype(F32) + rr[0:HD, :].astype(F32)).astype(BF)
    else:
        for out, own, got in ((to_right, dr, rl), (to_left, dl, rr)):
            out[0 : 2 * HD, :] = (own[...].astype(F32) + got[0 : 2 * HD, :].astype(F32)).astype(BF)
    if to_right.shape[0] > 2 * HD:
        to_right[2 * HD :, :] = rl[rl.shape[0] - EXTRA :, :]
        to_left[2 * HD :, :] = rr[rr.shape[0] - EXTRA :, :]


def send_body(yi, out_t, dqt, dkv, l4, r4, k0, k1, k2, k3, out, slots):
    y = yi[0]
    for i, ref in enumerate((k0, k1, k2, k3)):
        slots[(y + 4 - i) % 4] = ref[...]
    low = (((slots[0] + slots[1]) + slots[2]) + slots[3]).astype(BF)
    d = (dkv[...] + l4[0 : 2 * HD, :].astype(F32) + r4[0 : 2 * HD, :].astype(F32)).astype(BF)
    for s in range(NB):
        rows = slice(s * FD, (s + 1) * FD)
        out[s, 0:HD, :] = out_t[:, rows]
        out[s, HD : 2 * HD, :] = dqt[:, rows]
        out[s, 2 * HD : 4 * HD, :] = d[:, rows]
        out[s, 4 * HD :, :] = low


def done_body(r, out, dq, dk, dv, kg):
    for n, ref in enumerate((out, dq, dk, dv)):
        t = jnp.concatenate([r[h, n * HD : (n + 1) * HD, :] for h in range(NB)], axis=0)
        ref[...] = t.T
    for h in range(NB):
        whole = r[h, 4 * HD :, :].astype(F32)
        kg[:, h * HD : (h + 1) * HD] = whole[0:TAPS, 0:HD]


def shift(a, axis, by):
    n = lax.axis_size(axis)
    return lax.ppermute(a, axis, [(i, (i + by) % n) for i in range(n)])


def local(query, key_in, value, lengths, kernel, cotangent):
    z = lax.axis_index("z").astype(jnp.int32).reshape(1)
    head = lax.axis_index(("x", "c")).astype(jnp.int32).reshape(1)
    packed = call(pack_body, "pack", [sds((NB, 4 * HD, FD), BF)], [VM])(
        jnp.stack([query, cotangent, key_in, value])
    )[0]
    got = lax.all_to_all(packed, ("x", "c"), 0, 0, tiled=True)
    block_t = sds((2 * HD, ROWS), BF)
    wide_t = sds((2 * HD + EXTRA, ROWS), BF)
    kv, to_left = call(keys_body, "keys", [wide_t, wide_t], [VM])(got)
    kvl, kvr = [shift(kv, "z", 1)], [shift(to_left, "z", -1)]
    qa, cot, taps, flags = call(
        prep_body, "prep",
        [sds((ROWS, 2 * FD), BF), sds((ROWS, FD), BF), sds((32, FD), F32), sds((16,), jnp.int32)],
        [SM] * 3 + [VM] * 2, out_specs=[VM] * 3 + [SM],
    )(lengths, z, head, got, kernel)
    keys = (pltpu.VMEM((2 * FD, ROWS), BF), pltpu.VMEM((ROWS, FD), BF))
    queries = pltpu.VMEM((ROWS + 2 * HALO, 2 * FD), BF)
    unit = 2 * ROWS * ROWS * 256
    acc_t = sds((ROWS + 2 * HALO, FD), F32)
    acc = call(own_body, "attend_own", [acc_t], [VM] * 2, keys, flops=2 * unit, mib=20)(qa, kv)[0]
    for step in (1, 2, 3):
        acc, kvl[-1], kvr[-1] = lax.optimization_barrier((acc, kvl[-1], kvr[-1]))
        if step < 3:
            kvl.append(shift(kvl[-1], "z", 1))
            kvr.append(shift(kvr[-1], "z", -1))
        else:
            kf = shift(kvl[-1][0:HD], "z", 1)
            vf = shift(kvr[-1][HD : 2 * HD], "z", -1)
        own = (kv,) if step == 1 else ()
        acc = call(
            functools.partial(pair_body, step), f"attend_{step}", [acc_t],
            [SM] + [VM] * (6 + len(own)), keys + (queries,), flops=4 * unit, mib=20,
        )(flags, qa, kvl[0], kvr[0], kvl[step - 1], kvr[step - 1], acc, *own)[0]

    wide = ROWS + 2 * HALO
    out_t, kg, qb, qbt, gb, gbt = call(
        mid_body, "middle",
        [sds((HD, ROWS), BF), sds((32, FD), F32), sds((ROWS, 2 * FD), BF), sds((2 * FD, ROWS), BF),
         sds((ROWS, FD), BF), sds((FD, ROWS), BF)],
        [SM] + [VM] * 8,
        keys + (queries, pltpu.VMEM((wide, FD), F32), pltpu.VMEM((wide, FD), F32),
                pltpu.VMEM((wide, FD), F32), pltpu.VMEM((ROWS + HALO, FD), F32), pltpu.VMEM((32, FD), F32)),
        flops=3 * unit, mib=24,
    )(flags, qa, kvl[0], kvr[0], kf, vf, cot, taps, acc)

    back = (pltpu.VMEM((ROWS, 2 * FD), BF), pltpu.VMEM((ROWS, FD), BF))
    ops = (qb, qbt, gb, gbt)
    dq_t = sds((HD, ROWS), F32)
    half_t = sds((HD, ROWS), BF)
    dq, dk, dv = call(
        far_body, "back_far", [dq_t, half_t, half_t], [SM] + [VM] * 6, back, flops=5 * unit, mib=32
    )(flags, *ops, kf, vf)
    y = lax.axis_index("grp").astype(jnp.int32).reshape(1)
    far_t = sds((HD + EXTRA, ROWS), BF)
    mine, to_left = call(first_body, "first", [far_t, far_t], [VM] * 3)(dk, dv, kg)
    rl, rr = [shift(mine, "z", 1)], [shift(to_left, "z", -1)]
    for step in (3, 2, 1):
        dq, dl, dr = call(
            functools.partial(back_pair_body, step), f"back_{step}", [dq_t, block_t, block_t],
            [SM] + [VM] * 7, back, flops=10 * unit, mib=32,
        )(flags, *ops, kvl[step - 1], kvr[step - 1], dq)
        to_right, to_left = call(merge_body, f"merge_{step}", [wide_t if step > 1 else block_t] * 2, [VM] * 4)(
            dl, dr, rl[-1], rr[-1]
        )
        rl.append(shift(to_right, "z", 1))
        rr.append(shift(to_left, "z", -1))
    dqt, dkv = call(
        back_own_body, "back_own", [half_t, sds((2 * HD, ROWS), F32)], [VM] * 6,
        (pltpu.VMEM((HD, ROWS), F32),) + back, flops=5 * unit, mib=32,
    )(*ops, kv, dq)
    kg = call(line_body, "line", [sds((32, FD), F32)], [SM] + [VM] * 8, (pltpu.VMEM((NB, 32, FD), F32),))(
        z, mine, *rl[:3], shift(rl[2][2 * HD :], "z", 1), *rr[:3]
    )[0]
    kg, dqt = lax.optimization_barrier((kg, dqt))
    kgs = [kg] + [shift(kg, "grp", i) for i in (1, 2, 3)]
    packed = call(
        send_body, "pack_out", [sds((NB, 4 * HD + KG_ROWS, FD), BF)], [SM] + [VM] * 9,
        (pltpu.VMEM((4, 32, FD), F32),),
    )(y, out_t, dqt, dkv, rl[3], rr[3], *kgs)[0]
    got = lax.all_to_all(packed, ("x", "c"), 0, 0, tiled=True)
    frames = sds((FD, NB * HD), BF)
    outs = [frames] * 4 + [sds((TAPS, NB * HD), F32)]
    return tuple(call(done_body, "unpack_out", outs, [VM])(got))


def solution(mesh):
    fine = Mesh(mesh.devices.reshape(4, 8, 4, 2), ("grp", "z", "x", "c"))
    frames = P(("grp", "z", "x", "c"), None)
    return jax.shard_map(
        local,
        mesh=fine,
        in_specs=(frames, frames, frames, P("grp", None), P(), frames),
        out_specs=(frames, frames, frames, frames, P()),
        check_vma=False,
    )
```
